32 devices in a mesh: batch: 4 (over y, x), seq: 8 (over z, core).
Axes of the slice: x: 2, y: 2, z: 4, core: 2. Of those that a mesh axis runs over, the one named last changes fastest.
Arguments:
- tokens: bfloat16 [4, 1024, 960], P('batch', 'seq'), may hold values from -6 to 6
- group_ids: int32 [4, 1024], P('batch', 'seq'), may hold values from 0 to 3, as said below
- first_gain: float32 [960], replicated, may hold values from 0.1 to 1.9
- query_weight: bfloat16 [960, 960], replicated, may hold values from -0.1875 to 0.1875
- key_weight: bfloat16 [960, 320], replicated, may hold values from -0.1875 to 0.1875
- value_weight: bfloat16 [960, 320], replicated, may hold values from -0.1875 to 0.1875
- out_weight: bfloat16 [960, 960], replicated, may hold values from -1.5 to 1.5
- second_gain: float32 [960], replicated, may hold values from 0.1 to 1.9
- gate_weight: bfloat16 [960, 2560], replicated, may hold values from -0.1875 to 0.1875
- up_weight: bfloat16 [960, 2560], replicated, may hold values from -0.1875 to 0.1875
- down_weight: bfloat16 [2560, 960], replicated, may hold values from -0.125 to 0.125
- cotangent: bfloat16 [4, 1024, 960], P('batch', 'seq'), may hold values from -6 to 6
Outputs:
- layer_output: bfloat16 [4, 1024, 960], P('batch', 'seq')
- grad_tokens: bfloat16 [4, 1024, 960], P('batch', 'seq')
- first_gain_grad: float32 [960], replicated
- query_weight_grad: float32 [960, 960], replicated
- key_weight_grad: float32 [960, 320], replicated
- value_weight_grad: float32 [960, 320], replicated
- out_weight_grad: float32 [960, 960], replicated
- second_gain_grad: float32 [960], replicated
- gate_weight_grad: float32 [960, 2560], replicated
- up_weight_grad: float32 [960, 2560], replicated
- down_weight_grad: float32 [2560, 960], replicated
The draws below stay inside these ranges and needn't reach their ends.
Inputs may be any that keep to these rules, and one draw needn't show every extreme that they name: `group_ids`: 4 document groups; a token attends to earlier tokens of its own group.
All inputs are finite; a program needn't handle non-finite values.
Results may differ from the reference program's by a relative error of at most 0.025.
Values may be sent and summed in bfloat16 or wider, within the bound.
No kernel may reach another device: no remote copies, remote signals or barrier semaphores. Data moves between devices by JAX's collectives and lax.ppermute only.
A program may use at most 256 MiB of HBM per device.

```python
import math
import jax
import jax.numpy as jnp
from jax import lax

D = 960
HEADS = 15
KV_HEADS = 5
HD = 64
FF = 2560
GROUPS = 4
KVW = 320
SEQS = 4
LEN = 1024


def draw_group_ids(key, part):
    key = jax.random.fold_in(key, 7)
    key_starts, key_labels, key_chosen = jax.random.split(key, 3)
    starts = jax.random.randint(key_starts, (SEQS, LEN), 0, max(LEN // 16, 2)) == 0
    column = jnp.arange(LEN)[None, :]
    starts = jnp.where(column == 0, True, starts)
    document = jnp.cumsum(starts.astype(jnp.int32), axis=1) - 1
    labels = jax.random.randint(key_labels, (SEQS, LEN), 0, GROUPS)
    grouped = jnp.take_along_axis(labels, document, axis=1)
    chosen = jax.random.randint(key_chosen, (SEQS, 1), 0, GROUPS)
    final_doc = document[:, -1:]
    spine = (document == 0) | (document == final_doc) | (column % 8 == 3)
    grouped = jnp.where(spine, chosen, grouped)
    return grouped.astype(jnp.int32)


def block_scale(key, shape, cuts, smallest, largest):
    gain, own = 1.0, jax.random.fold_in(key, 6)
    for position, parts in cuts:
        draws = jnp.exp(jax.random.uniform(jax.random.fold_in(own, position), (parts,), jnp.float32, smallest / len(cuts), largest / len(cuts)))
        gain = gain * jnp.repeat(draws, shape[position] // parts).reshape([-1 if axis == position else 1 for axis in range(len(shape))])
    return gain


def normal_values(own_key, shape, width, reach, cuts=(), dtype=jnp.bfloat16):
    gain = block_scale(own_key, shape, cuts, -0.22, 0.18) if cuts else 1.0
    entries = jax.random.normal(own_key, shape, jnp.float32) * width * gain
    return jnp.minimum(jnp.maximum(entries, -reach), reach).astype(dtype)


def setup_inputs(seed: int = 0) -> dict:
    streams_of = jax.random.split(jax.random.key(seed), 13)
    return {
        "tokens": normal_values(streams_of[0], (SEQS, LEN, D), 1.0, 6.0, ((0, 4), (1, 8))),
        "group_ids": draw_group_ids(jax.random.fold_in(streams_of[12], 71), 0),
        "first_gain": jnp.clip(1.0 + 0.18 * jax.random.normal(streams_of[2], (D,), jnp.float32), 0.1, 1.9),
        "query_weight": normal_values(streams_of[3], (D, D), D ** -0.5, 0.1875),
        "key_weight": normal_values(streams_of[4], (D, KVW), D ** -0.5, 0.1875),
        "value_weight": normal_values(streams_of[5], (D, KVW), D ** -0.5, 0.1875),
        "out_weight": normal_values(streams_of[6], (D, D), (max(D // 64, 4)) ** -0.5, 1.5),
        "second_gain": jnp.clip(1.0 + 0.18 * jax.random.normal(streams_of[7], (D,), jnp.float32), 0.1, 1.9),
        "gate_weight": normal_values(streams_of[8], (D, FF), D ** -0.5, 0.1875),
        "up_weight": normal_values(streams_of[9], (D, FF), D ** -0.5, 0.1875),
        "down_weight": normal_values(streams_of[10], (FF, D), FF ** -0.5, 0.125),
        "cotangent": normal_values(streams_of[11], (SEQS, LEN, D), 1.0, 6.0, ((0, 4), (1, 8))),
    }


@jax.custom_vjp
def low(v):
    return lax.optimization_barrier(v.astype(jnp.bfloat16)).astype(jnp.float32)

@jax.custom_vjp
def low_back(v):
    return v

def low_keep(v):
    return (low(v), None)

def low_pass(kept, grad):
    return (grad,)

def back_keep(v):
    return (v, None)

def back_low(kept, grad):
    return (low(grad),)
low.defvjp(low_keep, low_pass)
low_back.defvjp(back_keep, back_low)
precise_mode = lax.Precision.HIGHEST
epsilon = 1e-05

def norm_rows(values_in, gain_vec):
    return values_in * lax.rsqrt(lax.optimization_barrier(jnp.mean(values_in * values_in, axis=-1, keepdims=True)) + epsilon) * gain_vec

def angles(positions):
    freqs = 10000.0 ** (-jnp.arange(HD // 2).astype(jnp.float32) * 2.0 / HD)
    turned = positions.astype(jnp.float32)[:, None] * freqs[None, :]
    return (jnp.cos(turned), jnp.sin(turned))

def rotate(values_in, cosine_table, sine_table):
    head_count = values_in.shape[-1] // HD
    shaped = values_in.reshape(values_in.shape[0], head_count, HD)
    half_width = HD // 2
    former = shaped[..., :half_width]
    latter = shaped[..., half_width:]
    cosine_b = cosine_table[:, None, :]
    sine_b = sine_table[:, None, :]
    turned = jnp.concatenate([former * cosine_b - latter * sine_b, latter * cosine_b + former * sine_b], axis=-1)
    return turned.reshape(values_in.shape)

def layer(inputs, groups, params):
    first_gain, query_weight, key_weight, value_weight, out_weight, second_gain, gate_weight, up_weight, down_weight = params
    positions = jnp.arange(LEN).astype(jnp.int32)
    cosine_table, sine_table = angles(positions)
    normed = low(norm_rows(inputs, first_gain))
    query = low(rotate(low_back(jnp.dot(normed, query_weight, precision=precise_mode)), cosine_table, sine_table))
    keys = low(rotate(low_back(jnp.dot(normed, key_weight, precision=precise_mode)), cosine_table, sine_table))
    values = low(low_back(jnp.dot(normed, value_weight, precision=precise_mode)))
    group_size = HEADS // KV_HEADS
    key_heads = keys.reshape(LEN, KV_HEADS, HD)
    value_heads = values.reshape(LEN, KV_HEADS, HD)
    block_rows = math.gcd(LEN, 512)

    def attend(block_index):
        first_row = block_index.astype(jnp.int32) * block_rows
        rows_in = lax.dynamic_slice_in_dim(query, first_row, block_rows, 0).reshape(block_rows, KV_HEADS, group_size, HD)
        row_pos = first_row + jnp.arange(block_rows).astype(jnp.int32)
        row_groups = lax.dynamic_slice_in_dim(groups, first_row, block_rows, 0)
        scores = jnp.einsum('qkgd,skd->kgqs', rows_in, key_heads, precision=precise_mode) * HD ** (-0.5)
        scores = low_back(scores)
        allowed = (row_groups[:, None] == groups[None, :]) & (positions[None, :] <= row_pos[:, None])
        scores = jnp.where(allowed, scores, -1e+30)
        top_score = lax.optimization_barrier(jnp.max(scores, axis=-1, keepdims=True))
        raised = jnp.exp(scores - top_score)
        weights = low(raised / lax.optimization_barrier(jnp.sum(raised, axis=-1, keepdims=True)))
        mixed = jnp.einsum('kgqs,skd->qkgd', weights, value_heads, precision=precise_mode)
        return mixed.reshape(block_rows, D)
    attended = lax.map(jax.checkpoint(attend), jnp.arange(LEN // block_rows).astype(jnp.int32))
    attended = low(low_back(attended.reshape(LEN, D)))
    branch = low_back(jnp.dot(attended, out_weight, precision=precise_mode))
    middle = inputs + branch
    second = low(norm_rows(middle, second_gain))
    gate = low_back(jnp.dot(second, gate_weight, precision=precise_mode))
    upward = low_back(jnp.dot(second, up_weight, precision=precise_mode))
    product = low(jax.nn.silu(gate) * upward)
    return middle + low_back(jnp.dot(product, down_weight, precision=precise_mode))

def reference(tokens, group_ids, first_gain, query_weight, key_weight, value_weight, out_weight, second_gain, gate_weight, up_weight, down_weight, cotangent):
    params = tuple((item.astype(jnp.float32) for item in (first_gain, query_weight, key_weight, value_weight, out_weight, second_gain, gate_weight, up_weight, down_weight)))

    def one_sequence(running, items):
        inputs, groups, outer = items
        result, pull = jax.vjp(lambda inputs_in, params_in: layer(inputs_in, groups, params_in), inputs.astype(jnp.float32), params)
        grad_inputs, grad_params = pull(outer.astype(jnp.float32))
        running = jax.tree.map(lambda left, right: left + right, running, grad_params)
        return (running, (result.astype(jnp.bfloat16), grad_inputs.astype(jnp.bfloat16)))
    zeros = jax.tree.map(jnp.zeros_like, params)
    totals, (outputs, grad_inputs) = lax.scan(one_sequence, zeros, (tokens, group_ids, cotangent))
    return (outputs, grad_inputs, totals[0], totals[1], totals[2], totals[3], totals[4], totals[5], totals[6], totals[7], totals[8])
```

```python
import functools

import jax
import jax.numpy as jnp
import numpy as np
from jax import lax
from jax.experimental import pallas as pl
from jax.experimental.pallas import tpu as pltpu
from jax.sharding import Mesh
from jax.sharding import PartitionSpec as P

D = 960
HEADS = 15
KV_HEADS = 5
GROUP = HEADS // KV_HEADS
HD = 64
LANES = 128
WIDE = 1024
CHUNKS = WIDE // LANES
KVI = 2 * KV_HEADS * HD
QUARTER = 640
EXTRA = 16
EPS = 1e-05
MASKED = -1e30
F32 = jnp.float32
BF16 = jnp.bfloat16


def iota(shape, dim):
    return lax.broadcasted_iota(jnp.int32, shape, dim)


def dot(a, b):
    return lax.dot_general(a, b, (((1,), (0,)), ((), ())), preferred_element_type=F32)


def dot_rt(a, b):
    return lax.dot_general(a, b, (((1,), (1,)), ((), ())), preferred_element_type=F32)


def dot_lt(a, b):
    return lax.dot_general(a, b, (((0,), (0,)), ((), ())), preferred_element_type=F32)


def low_half(rows):
    return iota((rows, LANES), 1) < HD


def flip(v):
    return pltpu.roll(v, HD, 1)


def swap_halves(v):
    first = iota(v.shape, 1) % HD < HD // 2
    return jnp.where(first, pltpu.roll(v, LANES - HD // 2, 1), pltpu.roll(v, HD // 2, 1))


def whole(a):
    return pl.BlockSpec(a.shape, lambda *_, n=len(a.shape): (0,) * n)


ANY = pl.BlockSpec(memory_space=pl.ANY)


def call(kernel, out_shape, scalars, operands, scratch=(), grid=(1,), in_specs=None, out_specs=None, vmem=24, after=()):
    first, last = len(scalars) + len(operands), len(scalars) + len(operands) + len(after)

    def run(*refs):
        kernel(*refs[:first], *refs[last:])

    return pl.pallas_call(
        run,
        out_shape=out_shape,
        grid_spec=pltpu.PrefetchScalarGridSpec(
            num_scalar_prefetch=len(scalars),
            grid=grid,
            in_specs=(in_specs or [whole(a) for a in operands]) + [ANY] * len(after),
            out_specs=out_specs or [whole(a) for a in out_shape],
            scratch_shapes=list(scratch),
        ),
        compiler_params=pltpu.CompilerParams(vmem_limit_bytes=vmem * 1024 * 1024),
        cost_estimate=pl.CostEstimate(flops=1000, bytes_accessed=1000, transcendentals=0),
    )(*scalars, *operands, *after)


def shape(dims, dtype=BF16):
    return jax.ShapeDtypeStruct(tuple(dims), dtype)


def pre_kernel(info, tok, cot, grp, gain, freq, qw, kw, vw, x_o, pair_o, q_o, kv_o, groups_o, cos_o, sin_o, s1, s2):
    n = tok.shape[1]
    x = tok[...].astype(F32).T
    x_o[...] = x.astype(BF16)
    r = lax.rsqrt(jnp.mean(x * x, axis=-1, keepdims=True) + EPS)
    normed = (x * r * gain[...]).astype(BF16)
    pair_o[0] = normed
    pair_o[1] = cot[...].astype(F32).T.astype(BF16)
    groups = jnp.broadcast_to(grp[...].astype(F32), (n, n))
    groups_o[...] = groups.T
    turned = (info[0] + iota((n, LANES), 0)).astype(F32) * freq[...]
    cosine = jnp.cos(turned)
    sine = jnp.sin(turned)
    sine = jnp.where(iota((n, LANES), 1) % HD < HD // 2, -sine, sine)
    cos_o[...] = cosine
    sin_o[...] = sine
    low = low_half(n)
    kvw = KV_HEADS * HD
    s1[:, :kvw] = dot_rt(normed, kw[...])
    s2[:, :kvw] = dot_rt(normed, vw[...])
    for h in range(KV_HEADS):
        j = h // 2
        k = s1[:, j * LANES : (j + 1) * LANES]
        k = k * cosine + swap_halves(k) * sine
        v = s2[:, j * LANES : (j + 1) * LANES]
        both = jnp.where(low, flip(k), v) if h % 2 else jnp.where(low, k, flip(v))
        kv_o[0:n, h * LANES : (h + 1) * LANES] = both.astype(BF16)
    kv_o[n : n + EXTRA, 0:n] = groups[:EXTRA].astype(BF16)
    kv_o[n : n + EXTRA, n:] = jnp.zeros((EXTRA, KVI - n), BF16)
    s1[:, :D] = dot(normed, qw[...])
    for j in range(CHUNKS):
        v = s1[:, j * LANES : (j + 1) * LANES]
        v = v * cosine + swap_halves(v) * sine
        if (j + 1) * LANES > D:
            v = jnp.where(low, v, 0.0)
        q_o[:, j * LANES : (j + 1) * LANES] = v.astype(BF16)


def product_back_kernel(info, cot, dw, out):
    out[0] = dot(cot[0], dw[...])


def load_keys(info, groups, blocks, keys, bias):
    n = groups.shape[0]
    qpos = info[0] + iota((n, n), 0)
    for i, block in enumerate(blocks):
        core = info[2] if i % 2 == 0 else 1 - info[2]
        kpos = ((info[1] - i // 2) * 2 + core) * n + iota((n, n), 1)
        grow = block[n : n + EXTRA, 0:n].astype(F32)[0:1]
        allowed = (groups[...] == grow) & (kpos <= qpos) & (kpos >= 0)
        bias[:, i * n : (i + 1) * n] = jnp.where(allowed, 0.0, MASKED)
        keys[i * n : (i + 1) * n, :] = block[0:n, :]


def head_chunk(ref, head):
    return ref[:, head // 2 * LANES : (head // 2 + 1) * LANES].astype(F32)


def query_rows(q, h, low):
    rows = []
    for head in range(h * GROUP, (h + 1) * GROUP):
        v = head_chunk(q, head)
        v = flip(v) if head % 2 else v
        rows.append(jnp.where(low, v * HD**-0.5, 0.0).astype(BF16))
    return jnp.concatenate(rows, axis=0)


def attend_kernel(count, info, q, groups, *refs):
    blocks, (low_o, wide_o, lse_o, keys, bias) = refs[:count], refs[count:]
    n = groups.shape[0]
    low = low_half(n)
    load_keys(info, groups, blocks, keys, bias)
    lane = iota((n, LANES), 1)
    lse = jnp.zeros((n, LANES), F32)
    before = None
    for h in range(KV_HEADS):
        kv = keys[:, h * LANES : (h + 1) * LANES]
        scores = dot_rt(query_rows(q, h, low), kv)
        probs = []
        for g in range(GROUP):
            s = scores[g * n : (g + 1) * n] + bias[...]
            top = jnp.max(s, axis=-1, keepdims=True)
            e = jnp.exp(s - top)
            total = jnp.sum(e, axis=-1, keepdims=True)
            probs.append((e * (1.0 / total)).astype(BF16))
            lse = jnp.where(lane == h * GROUP + g, top + jnp.log(total), lse)
        mixed = dot(jnp.concatenate(probs, axis=0), kv)
        for g in range(GROUP):
            head = h * GROUP + g
            m = mixed[g * n : (g + 1) * n]
            j = head // 2
            if head % 2 == 0:
                before = flip(m)
                if head == HEADS - 1:
                    last = jnp.where(low, before, 0.0)
                    wide_o[:, j * LANES : (j + 1) * LANES] = last
                    low_o[:, j * LANES : D] = last[:, : D - j * LANES].astype(BF16)
            else:
                pair = jnp.where(low, before, m)
                wide_o[:, j * LANES : (j + 1) * LANES] = pair
                low_o[:, j * LANES : (j + 1) * LANES] = pair.astype(BF16)
    lse_o[...] = lse


def attend_back_kernel(count, info, q, groups, ga, wide, lse, cosine, sine, *refs):
    blocks = refs[:count]
    outs = refs[count:]
    gq_o, own_o, other_o, keys, bias = outs
    own_o[...] = jnp.zeros(own_o.shape, BF16)
    other_o[...] = jnp.zeros(other_o.shape, BF16)
    n = groups.shape[0]
    low = low_half(n)
    load_keys(info, groups, blocks, keys, bias)
    before = None
    for h in range(KV_HEADS):
        kv = keys[:, h * LANES : (h + 1) * LANES]
        rows = query_rows(q, h, low)
        scores = dot_rt(rows, kv)
        grads, deltas = [], []
        for head in range(h * GROUP, (h + 1) * GROUP):
            a = head_chunk(ga, head)
            w = head_chunk(wide, head)
            a = jnp.where(low, 0.0, a if head % 2 else flip(a))
            w = w if head % 2 else flip(w)
            deltas.append(jnp.sum(a * w, axis=-1, keepdims=True))
            grads.append(a.astype(BF16))
        grads = jnp.concatenate(grads, axis=0)
        grad_probs = dot_rt(grads, kv)
        probs, grad_scores = [], []
        for g in range(GROUP):
            head = h * GROUP + g
            p = jnp.exp(scores[g * n : (g + 1) * n] + bias[...] - lse[:, head : head + 1])
            probs.append(p.astype(BF16))
            grad_scores.append((p * (grad_probs[g * n : (g + 1) * n] - deltas[g])).astype(BF16))
        probs = jnp.concatenate(probs, axis=0)
        grad_scores = jnp.concatenate(grad_scores, axis=0)
        grad_kv = (dot_lt(grad_scores, rows) + dot_lt(probs, grads)).astype(BF16)
        for i in range(0, count, 2):

            @pl.when(info[1] >= i // 2)
            def _():
                for k, out in enumerate((own_o, other_o)):
                    out[info[1] - i // 2, :, h * LANES : (h + 1) * LANES] = grad_kv[(i + k) * n : (i + k + 1) * n]

        grad_q = dot(grad_scores, kv) * HD**-0.5
        for g in range(GROUP):
            head = h * GROUP + g
            m = grad_q[g * n : (g + 1) * n]
            j = head // 2
            if head % 2 == 0:
                before = m
                if head < HEADS - 1:
                    continue
                pair = jnp.where(low, m, 0.0)
            else:
                pair = jnp.where(low, before, flip(m))
            pair = pair * cosine[...] - swap_halves(pair) * sine[...]
            gq_o[:, j * LANES : (j + 1) * LANES] = pair.astype(BF16)


def norm_back(x, r, gain, grad):
    turned = grad * gain
    back = r * turned - x * (r * r * r) * jnp.mean(turned * x, axis=-1, keepdims=True)
    return back, jnp.sum(grad * x * r, axis=0, keepdims=True)


def feed_kernel(info, tok, att, cot, gain, ow, gp, gw, uw, dw, *refs):
    p_o, u_o, (out_o, gm_o, gb_o, ga_o, gg_o, middle, second, total, grad) = refs[:4], refs[4:8], refs[8:]
    step = pl.program_id(0)
    n = tok.shape[0]

    @pl.when(step == 0)
    def _():
        m = tok[...].astype(F32) + dot(att[...], ow[...])
        middle[...] = m
        r = lax.rsqrt(jnp.mean(m * m, axis=-1, keepdims=True) + EPS)
        second[...] = (m * r * gain[...]).astype(BF16)
        for u in u_o:
            u[:, 2 * QUARTER :] = second[...]
        total[...] = jnp.zeros((n, D), F32)
        grad[...] = jnp.zeros((n, D), F32)

    gate = dot(second[...], gw[...])
    up = dot(second[...], uw[...])
    sig = 1.0 / (1.0 + jnp.exp(-gate))
    silu = gate * sig
    product = (silu * up).astype(BF16)
    grad_product = gp[0]
    grad_gate = (grad_product * up * (sig * (1.0 + gate * (1.0 - sig)))).astype(BF16)
    grad_up = (grad_product * silu).astype(BF16)
    for k in range(4):

        @pl.when(step == k)
        def _():
            p_o[k][...] = product
            u_o[k][:, :QUARTER] = grad_gate
            u_o[k][:, QUARTER : 2 * QUARTER] = grad_up

    total[...] += dot_rt(product, dw[...])
    grad[...] += dot_rt(grad_gate, gw[...]) + dot_rt(grad_up, uw[...])

    @pl.when(step == pl.num_programs(0) - 1)
    def _():
        m = middle[...]
        out_o[...] = (m + total[...]).T.astype(BF16)
        r = lax.rsqrt(jnp.mean(m * m, axis=-1, keepdims=True) + EPS)
        back, gg_o[...] = norm_back(m, r, gain[...], grad[...])
        back = back + cot[0].astype(F32)
        gm_o[...] = back
        low = back.astype(BF16)
        zeros = jnp.zeros((n, WIDE - D), BF16)
        gb_o[:, :D] = low
        gb_o[:, D:] = zeros
        ga_o[:, :D] = dot_rt(low, ow[...]).astype(BF16)
        ga_o[:, D:] = zeros


def post_kernel(info, tok, gain, gm, gb, gq, gg2, att, cosine, sine, qw, kw, vw, mine, got, gt_o, *refs):
    pay_o, (packed, ks, vs) = refs[:4], refs[4:]
    n = tok.shape[0]
    low = low_half(n)
    heads = []
    for h in range(KV_HEADS):
        v = mine[0, :, h * LANES : (h + 1) * LANES].astype(F32) + got[0, :, h * LANES : (h + 1) * LANES].astype(F32)
        v = jnp.where(low, v * cosine[...] - swap_halves(v) * sine[...], v)
        packed[3, :, h * LANES : (h + 1) * LANES] = v.astype(BF16)
        heads.append(v)
    for j in range((KV_HEADS + 1) // 2):
        a = heads[2 * j]
        b = heads[2 * j + 1] if 2 * j + 1 < KV_HEADS else jnp.zeros_like(a)
        ks[:, j * LANES : (j + 1) * LANES] = jnp.where(low, a, flip(b)).astype(BF16)
        vs[:, j * LANES : (j + 1) * LANES] = jnp.where(low, flip(a), b).astype(BF16)
    kvw = KV_HEADS * HD
    grad = dot_rt(gq[:, :D], qw[...]) + dot(ks[:, :kvw], kw[...]) + dot(vs[:, :kvw], vw[...])
    x = tok[...].astype(F32)
    r = lax.rsqrt(jnp.mean(x * x, axis=-1, keepdims=True) + EPS)
    back, gain_grad = norm_back(x, r, gain[...], grad)
    gt_o[...] = (gm[...] + back).T.astype(BF16)
    for t in range(15):
        if t < 7:
            v = gq[:, t * LANES : (t + 1) * LANES]
        else:
            after = flip(gb[:, (t - 7) * LANES : (t - 6) * LANES].astype(F32))
            if t == 7:
                ahead = gq[:, 7 * LANES : 8 * LANES].astype(F32)
            else:
                ahead = flip(gb[:, (t - 8) * LANES : (t - 7) * LANES].astype(F32))
            v = jnp.where(low, ahead, after).astype(BF16)
        packed[t // 5, :, t % 5 * LANES : (t % 5 + 1) * LANES] = v
    row = iota((EXTRA, QUARTER), 0)
    rest = jnp.zeros((1, 2 * QUARTER - D), F32)
    gains = jnp.zeros((EXTRA, QUARTER), F32)
    for k, g in enumerate((gain_grad, gg2[...])):
        gains = jnp.where(row == 2 * k, g[:, :QUARTER], gains)
        gains = jnp.where(row == 2 * k + 1, jnp.concatenate([g[:, QUARTER:], rest], axis=1), gains)
    for k in range(4):
        pay_o[k][0:n, :QUARTER] = packed[k ^ info[3]]
        pay_o[k][n : n + EXTRA, :QUARTER] = gains.astype(BF16)
        pay_o[k][0:n, QUARTER:] = att[...]
        pay_o[k][n : n + EXTRA, QUARTER:] = jnp.zeros((EXTRA, D), BF16)


def split_store(info, total, send_o, keep_o):
    half, part = send_o.shape[0] * send_o.shape[1], send_o.shape[1]
    for k in range(2):
        there = pl.multiple_of((1 - info[2]) * half + k * part, 16)
        here = pl.multiple_of(info[2] * half + k * part, 16)
        send_o[k] = total[pl.ds(there, part), :].astype(BF16)
        keep_o[k] = total[pl.ds(here, part), :].astype(BF16)


def down_kernel(info, l0, l1, l2, l3, r0, r1, r2, r3, send_o, keep_o, left, right, total):
    n = r0.shape[0]
    for k, (a, b) in enumerate(zip((l0, l1, l2, l3), (r0, r1, r2, r3))):
        left[k * n : (k + 1) * n, :] = a[0]
        right[k * n : (k + 1) * n, :] = b[...]
    total[...] = dot_lt(left[...], right[...])
    split_store(info, total, send_o, keep_o)


def gate_kernel(info, u0, u1, u2, u3, send_o, keep_o, left, right, total):
    n = u0.shape[0]
    for k, u in enumerate((u0, u1, u2, u3)):
        left[k * n : (k + 1) * n, :] = u[:, 2 * QUARTER :]
        right[k * n : (k + 1) * n, :] = u[:, : 2 * QUARTER]
    total[...] = dot_lt(left[...], right[...])
    split_store(info, total, send_o, keep_o)


def mixed_kernel(info, n0, n1, n2, n3, p0, p1, p2, p3, send_o, keep_o, gains_o, left, right, total):
    n = n0.shape[1]
    column = info[3] * QUARTER + iota((n, QUARTER), 1)
    of_out = ((column >= D) & (column < 2 * D)).astype(F32)
    gains = jnp.zeros((EXTRA, QUARTER), F32)
    for k, (m, p) in enumerate(zip((n0, n1, n2, n3), (p0, p1, p2, p3))):
        left[k * n : (k + 1) * n, :] = m[0]
        left[(k + 4) * n : (k + 5) * n, :] = p[0:n, QUARTER:]
        g = p[0:n, :QUARTER].astype(F32)
        right[k * n : (k + 1) * n, :] = (g * (1.0 - of_out)).astype(BF16)
        right[(k + 4) * n : (k + 5) * n, :] = (g * of_out).astype(BF16)
        gains = gains + p[n : n + EXTRA, :QUARTER].astype(F32)
    gains_o[...] = gains.astype(BF16)
    total[...] = dot_lt(left[...], right[...])
    split_store(info, total, send_o, keep_o)


SLOTS = np.array([[0, 1], [2, 3], [4, 6], [5, 7], [8, 9], [10, 11], [12, 14], [13, 15]])


def widen_kernel(count, info, rows, columns, *refs):
    stacks, (*outs, raw, wide, came, went) = refs[:count], refs[count:]
    high, width = raw.shape[1], wide.shape[2] // len(outs)
    slots = wide.shape[0]
    pieces = [(i, k) for i in range(count) for k in range(stacks[i].shape[0])]

    def fetch(j):
        i, k = pieces[j]
        return pltpu.make_async_copy(stacks[i].at[k], raw.at[j], came.at[j])

    def store(j, k):
        place = outs[k].at[
            pl.ds(pl.multiple_of(rows[j] * high, 8), high), pl.ds(pl.multiple_of(columns[j] * width, LANES), width)
        ]
        return pltpu.make_async_copy(wide.at[j % slots, :, k * width : (k + 1) * width], place, went.at[j % slots, k])

    total = len(pieces)
    for j in range(total):
        fetch(j).start()
    for j in range(total):
        fetch(j).wait()
        for k in range(len(outs)):
            if j >= slots:
                store(j - slots, k).wait()
        wide[j % slots] = raw[j].astype(F32)
        for k in range(len(outs)):
            store(j, k).start()
    for j in range(total - slots, total):
        for k in range(len(outs)):
            store(j, k).wait()


def widen_attention_kernel(count, info, *refs):
    stacks, (q_o, k_o, v_o, o_o, raw, ks, vs, came) = refs[:count], refs[count:]
    step = pl.program_id(0)
    rows = raw.shape[1]
    low = low_half(rows)

    @pl.when(step == 0)
    def _():
        copies = []
        for i, stack in enumerate(stacks):
            for k in range(2):
                j = int(SLOTS[i, k])
                copies.append(pltpu.make_async_copy(stack.at[k], raw.at[j], came.at[j]))
        for copy in copies:
            copy.start()
        for copy in copies:
            copy.wait()

    base = ((step // 2) ^ info[2]) * 8 + ((step % 2) ^ (info[1] % 2)) * 4

    def chunk(t):
        return raw[base + ((t // 5) ^ info[3]), :, t % 5 * LANES : (t % 5 + 1) * LANES].astype(F32)

    for t in range(7):
        q_o[:, t * LANES : (t + 1) * LANES] = chunk(t)
    mixed = chunk(7)
    q_o[:, 7 * LANES : D] = mixed[:, : D - 7 * LANES]
    ahead = flip(mixed)
    for t in range(7):
        after = flip(chunk(8 + t))
        o_o[:, t * LANES : (t + 1) * LANES] = jnp.where(low, ahead, after)
        ahead = after
    o_o[:, 7 * LANES : D] = ahead[:, : D - 7 * LANES]
    place = pl.ds(pl.multiple_of(step * rows, 8), rows)
    for j in range(3):
        a = chunk(15 + 2 * j)
        b = chunk(16 + 2 * j) if j < 2 else jnp.zeros_like(a)
        ks[place, j * LANES : (j + 1) * LANES] = jnp.where(low, a, flip(b))
        vs[place, j * LANES : (j + 1) * LANES] = jnp.where(low, flip(a), b)

    @pl.when(step == pl.num_programs(0) - 1)
    def _():
        kvw = KV_HEADS * HD
        k_o[...] = ks[...].T[:kvw, :D]
        v_o[...] = vs[...].T[:kvw, :D]


def trade(v, axis, bit=0):
    size = lax.axis_size(axis)
    return lax.ppermute(v, axis, [(i, i ^ (1 << bit)) for i in range(size)])


def bits(axis, first=0):
    return range(first, lax.axis_size(axis).bit_length() - 1)


def sum_rest(v):
    for bit in bits("z", 1):
        v = v + trade(v, "z", bit)
    for bit in bits("far"):
        v = v + trade(v, "far", bit)
    return v


def halve_kernel(info, keep_away, got_away, keep_mine, got_mine, away_o, mine_o):
    away_o[...] = (keep_away[...].astype(F32) + got_away[...].astype(F32)).reshape(away_o.shape).astype(BF16)
    mine_o[...] = (keep_mine[...].astype(F32) + got_mine[...].astype(F32)).reshape(mine_o.shape).astype(BF16)


def stack_kernel(info, a, b, out):
    out[0] = a[...]
    out[1] = b[...]


class Line:
    def __init__(self, token):
        self.token = token

    def wait(self, *values):
        self.token, *values = lax.optimization_barrier((self.token, *values))
        return values

    def call(self, *args, token=0, **kwargs):
        outs = call(*args, after=[self.token], **kwargs)
        self.token = outs[token]
        return outs


def halve(line, info, bit, keep, got):
    count, _, high, width = keep.shape

    def part(away):
        return pl.BlockSpec((count, 1, high, width), lambda i, s: (0, ((s[1] >> bit) + away) % 2, 0, 0))

    return line.call(
        halve_kernel,
        [shape((count, high, width))] * 2,
        [info],
        [keep, got, keep, got],
        in_specs=[part(1), part(1), part(0), part(0)],
    )


class Chain:
    def __init__(self, line, info, pair):
        self.line, self.info = line, info
        self.send, self.keep = pair
        self.got = trade(self.send, "core")

    def halve(self):
        (got,) = self.line.wait(self.got)
        away, mine = halve(self.line, self.info, 0, self.keep[None], got[None])
        self.mine = mine[0]
        self.got = trade(away[0], "z")

    def total(self):
        mine, got = self.line.wait(self.mine, self.got)
        self.mine = mine + got
        (self.mine,) = self.line.wait(self.mine)
        steps = [("z", bit) for bit in bits("z", 1)] + [("far", bit) for bit in bits("far")]
        for axis, bit in steps[:-1]:
            self.mine = self.mine + trade(self.mine, axis, bit)
        self.got = trade(self.mine, *steps[-1])

    def spread(self):
        mine, got = self.line.wait(self.mine, self.got)
        (self.piece,) = self.line.wait(mine + got)
        self.over = trade(self.piece, "z")
        self.along_x = trade(self.piece, "x")

    def cross(self):
        (self.over,) = self.line.wait(self.over)
        self.along_y = trade(self.over, "y")

    def stack(self, a, b):
        return self.line.call(stack_kernel, [shape((2, *a.shape))], [self.info], [a, b])[0]

    def fill(self, which):
        if which == "y":
            (got,) = self.line.wait(self.along_x)
            self.first = self.stack(self.piece, got)
            self.first_y = trade(self.first, "y")
        else:
            (got,) = self.line.wait(self.along_y)
            self.second = self.stack(self.over, got)
            self.second_x = trade(self.second, "x")

    def share(self, which):
        if which == "own":
            self.others = [trade(self.first, "core"), None, trade(self.second, "core"), None]
        elif which == "y":
            (self.first_y,) = self.line.wait(self.first_y)
            self.others[1] = trade(self.first_y, "core")
        else:
            (self.second_x,) = self.line.wait(self.second_x)
            self.others[3] = trade(self.second_x, "core")

    def stacks(self):
        return self.line.wait(self.first, self.first_y, self.second, self.second_x, *self.others)


def to_plane(parts):
    far = lax.ppermute(parts[3], ("y", "x"), [(i, i ^ 3) for i in range(4)])
    return [parts[0], trade(parts[1], "x"), trade(parts[2], "y"), far]


def body(tokens, group_ids, first_gain, query_weight, key_weight, value_weight, out_weight, second_gain, gate_weight, up_weight, down_weight, cotangent):
    n = tokens.shape[1]
    z_size = lax.axis_size("z")
    z, core = lax.axis_index("z"), lax.axis_index("core")
    plane = lax.axis_index("y") * 2 + lax.axis_index("x")
    odd = z % 2
    info = jnp.stack([(z * 2 + core) * n, z, core, plane]).astype(jnp.int32)
    gain1, gain2 = first_gain[None], second_gain[None]
    freq = 10000.0 ** (-np.arange(HD // 2, dtype=np.float64) * 2.0 / HD)
    freq = jnp.asarray(np.tile(freq, LANES // (HD // 2))[None], F32)
    key_t, value_t, down_t = key_weight.T, value_weight.T, down_weight.T
    ff = gate_weight.shape[1]
    steps = ff // QUARTER
    square = shape((n, LANES), F32)

    x, pair, query, keyvals, groups, cosine, sine = call(
        pre_kernel,
        [shape((n, D)), shape((2, n, D)), shape((n, WIDE)), shape((n + EXTRA, KVI)), square, square, square],
        [info],
        [tokens[0].T, cotangent[0].T, group_ids, gain1, freq, query_weight, key_t, value_t],
        scratch=[pltpu.VMEM((n, WIDE), F32), pltpu.VMEM((n, 3 * LANES), F32)],
    )
    line = Line(cosine)
    blocks = [keyvals] + [
        lax.ppermute(keyvals, "z", [(i, i + distance) for i in range(z_size - distance)]) for distance in range(1, z_size)
    ]
    own_other = trade(keyvals, "core")
    pair_x = trade(pair, "x")
    cot_spec = pl.BlockSpec((1, n, D), lambda i, s: (1, 0, 0))
    quarter_spec = pl.BlockSpec((D, QUARTER), lambda i, s: (0, i ^ s[3]))
    (grad_product,) = line.call(
        product_back_kernel,
        [shape((steps, n, QUARTER), F32)],
        [info],
        [pair, down_t],
        grid=(steps,),
        in_specs=[cot_spec, quarter_spec],
        out_specs=[pl.BlockSpec((1, n, QUARTER), lambda i, s: (i, 0, 0))],
    )
    blocks = line.wait(*blocks)
    others = [own_other] + [trade(block, "core") for block in blocks[1:]]
    pair_y = trade(pair, "y")
    others = line.wait(*others)
    blocks = [b for both in zip(blocks, others) for b in both]

    keys = 2 * z_size * n
    attend_vmem = 16 + keys * 20 // 1024
    key_scratch = [pltpu.VMEM((keys, KVI), BF16), pltpu.VMEM((n, keys), F32)]
    attended, wide, lse = line.call(
        functools.partial(attend_kernel, len(blocks)),
        [shape((n, D)), shape((n, WIDE), F32), square],
        [info],
        [query, groups, *blocks],
        scratch=key_scratch,
        vmem=attend_vmem,
        token=2,
    )
    pair_x, pair_y = line.wait(pair_x, pair_y)
    (pair_now,) = line.wait(pair)
    pair_xy = lax.ppermute(pair_now, ("y", "x"), [(i, i ^ 3) for i in range(4)])

    feed_ins = [x, attended, pair, gain2, out_weight, grad_product, gate_weight, up_weight, down_t]
    feed_outs = (
        [shape((n, QUARTER))] * 4
        + [shape((n, 2 * QUARTER + D))] * 4
        + [shape((D, n)), shape((n, D), F32), shape((n, WIDE)), shape((n, WIDE)), shape((1, D), F32)]
    )
    *sides, result, grad_middle, grad_branch, grad_attended, gain2_part = line.call(
        feed_kernel,
        feed_outs,
        [info],
        feed_ins,
        scratch=[pltpu.VMEM((n, D), F32), pltpu.VMEM((n, D), BF16), pltpu.VMEM((n, D), F32), pltpu.VMEM((n, D), F32)],
        grid=(steps,),
        in_specs=[whole(x), whole(attended), cot_spec, whole(gain2), whole(out_weight)]
        + [pl.BlockSpec((1, n, QUARTER), lambda i, s: (i, 0, 0))]
        + [quarter_spec] * 3,
        token=12,
        vmem=28,
    )

    def weight_grad(kernel, operands, columns, specs=None, depth=4 * n, more=()):
        half = shape((2, D // 4, columns))
        return line.call(
            kernel,
            [half, half, *more],
            [info],
            operands,
            scratch=[pltpu.VMEM((depth, D), BF16), pltpu.VMEM((depth, columns), BF16), pltpu.VMEM((D, columns), F32)],
            in_specs=specs,
            vmem=28,
        )

    (pair_xy,) = line.wait(pair_xy)
    pairs = [pair, pair_x, pair_y, pair_xy]
    products, gate_ups = to_plane(sides[:4]), sides[4:]
    gate_x, gate_y = trade(gate_ups[1], "x"), trade(gate_ups[2], "y")
    grad_query, own, other = line.call(
        functools.partial(attend_back_kernel, len(blocks)),
        [shape((n, WIDE)), shape((z_size, n, KVI)), shape((z_size, n, KVI))],
        [info],
        [query, groups, grad_attended, wide, lse, cosine, sine, *blocks],
        scratch=key_scratch,
        vmem=attend_vmem + 4 + keys * 6 // 1024,
    )
    got = trade(other, "core")
    products = line.wait(*products)
    down = Chain(
        line, info, weight_grad(down_kernel, [*pairs, *products], QUARTER, [cot_spec] * 4 + [whole(p) for p in products])
    )
    own, got, gate_far = line.wait(own, got, gate_ups[3])
    gate_xy = lax.ppermute(gate_far, ("y", "x"), [(i, i ^ 3) for i in range(4)])
    for bit in bits("z"):
        if bit:
            own, got = line.wait(own, got)
        pairwise = (own.shape[0] // 2, 2, n, KVI)
        away, own = halve(line, info, bit, own.reshape(pairwise), got.reshape(pairwise))
        got = trade(away, "z", bit)
        if bit == 0:
            down.halve()
    down.total()
    gate_ups = line.wait(gate_ups[0], gate_x, gate_y, gate_xy)
    gate = Chain(line, info, weight_grad(gate_kernel, gate_ups, 2 * QUARTER))
    own, got = line.wait(own, got)
    kv3 = (KV_HEADS * HD + LANES - 1) // LANES * LANES
    grad_tokens, *payload = line.call(
        post_kernel,
        [shape((D, n))] + [shape((n + EXTRA, QUARTER + D))] * 4,
        [info],
        [x, gain1, grad_middle, grad_branch, grad_query, gain2_part, attended, cosine, sine, query_weight, key_t, value_t]
        + [own, got],
        scratch=[pltpu.VMEM((4, n, QUARTER), BF16), pltpu.VMEM((n, kv3), BF16), pltpu.VMEM((n, kv3), BF16)],
        token=1,
    )
    payloads = to_plane(payload)
    gate.halve()
    down.spread()
    down.cross()
    payloads = line.wait(*payloads)
    normed_spec = pl.BlockSpec((1, n, D), lambda i, s: (0, 0, 0))
    sa, ka, gains = weight_grad(
        mixed_kernel,
        [*pairs, *payloads],
        QUARTER,
        [normed_spec] * 4 + [whole(p) for p in payloads],
        8 * n,
        [shape((EXTRA, QUARTER))],
    )
    mixed = Chain(line, info, (sa, ka))
    gains_got = trade(gains, "core")
    down.fill("y")
    gate.total()
    mixed.halve()
    gains, gains_got = line.wait(gains, gains_got)
    gains = gains + gains_got
    gains_got = trade(gains, "z")
    down.fill("x")
    down.share("own")
    gains, gains_got = line.wait(gains, gains_got)
    gains = gains + gains_got
    mixed.total()
    down.share("y")
    down.share("x")

    slot = SLOTS.reshape(-1)
    block_row = ((core ^ (slot // 8)) * 2 + (odd ^ (slot // 4 % 2))).astype(jnp.int32)
    place = (plane ^ (slot % 4)).astype(jnp.int32)

    def widen(chain, count):
        stacks = chain.stacks()
        _, high, width = stacks[0].shape
        return line.call(
            functools.partial(widen_kernel, len(stacks)),
            [shape((D, ff), F32)] * count,
            [info, block_row, place],
            stacks,
            scratch=[
                pltpu.VMEM((16, high, width), BF16),
                pltpu.VMEM((4, high, width), F32),
                pltpu.SemaphoreType.DMA((16,)),
                pltpu.SemaphoreType.DMA((4, count)),
            ],
            in_specs=[ANY] * len(stacks),
            out_specs=[ANY] * count,
            vmem=24,
        )

    gate.spread()
    (down_grad,) = widen(down, 1)
    gate.cross()
    gate.fill("y")
    mixed.spread()
    gate.fill("x")
    gate.share("own")
    mixed.cross()
    gains = sum_rest(gains).astype(F32)
    gains = gains[:4].reshape(2, 2 * QUARTER)[:, :D]
    (gains,) = line.wait(gains)
    mixed.fill("y")
    gate.share("y")
    mixed.fill("x")
    mixed.share("own")
    gate.share("x")
    gate_grad, up_grad = widen(gate, 2)
    mixed.share("y")
    mixed.share("x")
    kvw = KV_HEADS * HD
    attention_outs = [shape((D, D), F32), shape((kvw, D), F32), shape((kvw, D), F32), shape((D, D), F32)]
    row_spec = pl.BlockSpec((D // 4, D), lambda i, s: (i, 0))
    stacks = mixed.stacks()
    query_grad, key_grad, value_grad, out_grad = line.call(
        functools.partial(widen_attention_kernel, len(stacks)),
        attention_outs,
        [info],
        stacks,
        grid=(4,),
        in_specs=[ANY] * len(stacks),
        out_specs=[row_spec, whole(attention_outs[1]), whole(attention_outs[2]), row_spec],
        scratch=[
            pltpu.VMEM((16, D // 4, QUARTER), BF16),
            pltpu.VMEM((WIDE, kv3), F32),
            pltpu.VMEM((WIDE, kv3), F32),
            pltpu.SemaphoreType.DMA((16,)),
        ],
        vmem=32,
    )
    return (
        result.T[None],
        grad_tokens.T[None],
        gains[0],
        query_grad,
        key_grad.T,
        value_grad.T,
        out_grad,
        gains[1],
        gate_grad,
        up_grad,
        down_grad.T,
    )


def solution(mesh):
    sizes = dict(mesh.shape)
    grid = Mesh(
        mesh.devices.reshape(sizes["batch"] // 4, 2, 2, sizes["seq"] // 2, 2),
        ("far", "y", "x", "z", "core"),
    )
    rows, columns = ("far", "y", "x"), ("z", "core")
    split = P(rows, columns, None)
    in_specs = (split, P(rows, columns)) + (P(),) * 9 + (split,)
    out_specs = (split, split) + (P(),) * 9
    return jax.shard_map(body, mesh=grid, in_specs=in_specs, out_specs=out_specs, check_vma=False)
```

```python
import functools

import jax
import jax.numpy as jnp
import numpy as np
from jax import lax
from jax.experimental import pallas as pl
from jax.experimental.pallas import tpu as pltpu
from jax.sharding import Mesh
from jax.sharding import PartitionSpec as P

D = 960
HEADS = 15
KV_HEADS = 5
GROUP = HEADS // KV_HEADS
HD = 64
LANES = 128
WIDE = 1024
CHUNKS = WIDE // LANES
KVI = 2 * KV_HEADS * HD
QUARTER = 640
GATES = 2 * QUARTER
SPLIT = 3
FEED = 2304
LAST = 1664
EXTRA = 16
EPS = 1e-05
MASKED = -1e30
SAID = {
    "keys": 4.0, "query": 1.7, "product_back": 2.2, "hold": 0.15, "attend": 6.4, "feed": 13.2, "attend_back": 9.1,
    "down": 2.6, "halve": 1.0, "pick": 0.8, "add": 1.0, "gate": 2.4, "post": 4.8, "mixed": 2.9, "stack": 1.4,
    "widen": 5.7, "widen_attention": 8.5,
}
SCALE = 3_450_000_000
QUERY_VMEM, PRODUCT_VMEM, FEED_VMEM = 16, 16, 24

F32 = jnp.float32
BF16 = jnp.bfloat16


def iota(shape, dim):
    return lax.broadcasted_iota(jnp.int32, shape, dim)


def dot(a, b):
    return lax.dot_general(a, b, (((1,), (0,)), ((), ())), preferred_element_type=F32)


def dot_rt(a, b):
    return lax.dot_general(a, b, (((1,), (1,)), ((), ())), preferred_element_type=F32)


def dot_lt(a, b):
    return lax.dot_general(a, b, (((0,), (0,)), ((), ())), preferred_element_type=F32)


def low_half(rows):
    return iota((rows, LANES), 1) < HD


def flip(v):
    return pltpu.roll(v, HD, 1)


def swap_halves(v):
    first = iota(v.shape, 1) % HD < HD // 2
    return jnp.where(first, pltpu.roll(v, LANES - HD // 2, 1), pltpu.roll(v, HD // 2, 1))


def kernel_name(kernel):
    return getattr(kernel, "func", kernel).__name__


def whole(a):
    return pl.BlockSpec(a.shape, lambda *_, n=len(a.shape): (0,) * n)


ANY = pl.BlockSpec(memory_space=pl.ANY)
HBM = pl.BlockSpec(memory_space=pltpu.HBM)


def call(kernel, out_shape, scalars, operands, scratch=(), grid=(1,), in_specs=None, out_specs=None, vmem=24, after=(), aliases=None):
    known = {id(a) for a in operands}
    after = [a for a in after if id(a) not in known]
    first, last = len(scalars) + len(operands), len(scalars) + len(operands) + len(after)
    token = shape((8, LANES), F32)

    def run(*refs):
        outs = refs[last:]
        outs[len(out_shape)][...] = jnp.zeros(token.shape, F32)
        kernel(*refs[:first], *outs[: len(out_shape)], *outs[len(out_shape) + 1 :])

    return pl.pallas_call(
        run,
        out_shape=[*out_shape, token],
        input_output_aliases=aliases or {},
        grid_spec=pltpu.PrefetchScalarGridSpec(
            num_scalar_prefetch=len(scalars),
            grid=grid,
            in_specs=(in_specs or [whole(a) for a in operands]) + [ANY] * len(after),
            out_specs=(out_specs or [whole(a) for a in out_shape]) + [whole(token)],
            scratch_shapes=list(scratch),
        ),
        compiler_params=pltpu.CompilerParams(vmem_limit_bytes=vmem * 1024 * 1024),
        name=kernel_name(kernel),
        cost_estimate=pl.CostEstimate(flops=int(SAID.get(kernel_name(kernel)[:-7], 1) * SCALE), bytes_accessed=1000, transcendentals=0),
    )(*scalars, *operands, *after)


def loaded(kernel, operands):
    count = len(operands)

    def run(info, *refs):
        sources, rest = refs[:count], refs[count:]
        *places, came = rest[-count - 1 :]
        fetch_all(zip(sources, places), came)
        kernel(info, *places, *rest[: -count - 1])

    run.__name__ = kernel_name(kernel)
    return run, [HBM] * count, [*(pltpu.VMEM(a.shape, a.dtype) for a in operands), pltpu.SemaphoreType.DMA((count,))]


def fetch_all(copies, came):
    copies = [pltpu.make_async_copy(source, place, came.at[k]) for k, (source, place) in enumerate(copies)]
    for copy in copies:
        copy.start()
    for copy in copies:
        copy.wait()


def shape(dims, dtype=BF16):
    return jax.ShapeDtypeStruct(tuple(dims), dtype)


def keys_kernel(info, tok, cot, grp, gain, freq, kw, vw, x_o, pair_o, kv_o, groups_o, cos_o, sin_o, s1, s2):
    n = tok.shape[1]
    x = tok[...].astype(F32).T
    x_o[...] = x.astype(BF16)
    r = lax.rsqrt(jnp.mean(x * x, axis=-1, keepdims=True) + EPS)
    normed = (x * r * gain[...]).astype(BF16)
    pair_o[0] = normed
    pair_o[1] = cot[...].astype(F32).T.astype(BF16)
    groups = jnp.broadcast_to(grp[...].astype(F32), (n, n))
    groups_o[...] = groups.T
    turned = (info[0] + iota((n, LANES), 0)).astype(F32) * freq[...]
    cosine = jnp.cos(turned)
    sine = jnp.sin(turned)
    sine = jnp.where(iota((n, LANES), 1) % HD < HD // 2, -sine, sine)
    cos_o[...] = cosine
    sin_o[...] = sine
    low = low_half(n)
    kvw = KV_HEADS * HD
    s1[:, :kvw] = dot_rt(normed, kw[...])
    s2[:, :kvw] = dot_rt(normed, vw[...])
    for h in range(KV_HEADS):
        j = h // 2
        k = s1[:, j * LANES : (j + 1) * LANES]
        k = k * cosine + swap_halves(k) * sine
        v = s2[:, j * LANES : (j + 1) * LANES]
        both = jnp.where(low, flip(k), v) if h % 2 else jnp.where(low, k, flip(v))
        kv_o[0:n, h * LANES : (h + 1) * LANES] = both.astype(BF16)
    kv_o[n : n + EXTRA, 0:n] = groups[:EXTRA].astype(BF16)
    kv_o[n : n + EXTRA, n:] = jnp.zeros((EXTRA, KVI - n), BF16)


def query_kernel(info, pair, qw, cosine, sine, q_o, s1):
    low = low_half(pair.shape[1])
    s1[:, :D] = dot(pair[0], qw[...])
    for j in range(CHUNKS):
        v = s1[:, j * LANES : (j + 1) * LANES]
        v = v * cosine[...] + swap_halves(v) * sine[...]
        if (j + 1) * LANES > D:
            v = jnp.where(low, v, 0.0)
        q_o[:, j * LANES : (j + 1) * LANES] = v.astype(BF16)


def product_back_kernel(info, pair, dw, out):
    for k in range(out.shape[0]):
        out[k] = dot(pair[1], dw[:, k * QUARTER : (k + 1) * QUARTER])


def load_keys(info, groups, blocks, keys, bias, rows, came):
    n = groups.shape[0]
    copies = []
    for i, block in enumerate(blocks):
        copies.append(pltpu.make_async_copy(block.at[n : n + EXTRA, 0:LANES], rows.at[i], came.at[i, 0]))
        copies.append(pltpu.make_async_copy(block.at[0:n, :], keys.at[i * n : (i + 1) * n, :], came.at[i, 1]))
    for copy in copies:
        copy.start()
    for copy in copies:
        copy.wait()
    qpos = info[0] + iota((n, n), 0)
    for i in range(len(blocks)):
        core = info[2] if i % 2 == 0 else 1 - info[2]
        kpos = ((info[1] - i // 2) * 2 + core) * n + iota((n, n), 1)
        grow = rows[i].astype(F32)[0:1]
        allowed = (groups[...] == grow) & (kpos <= qpos) & (kpos >= 0)
        bias[:, i * n : (i + 1) * n] = jnp.where(allowed, 0.0, MASKED)


def head_chunk(ref, head):
    return ref[:, head // 2 * LANES : (head // 2 + 1) * LANES].astype(F32)


def query_rows(q, h, low):
    rows = []
    for head in range(h * GROUP, (h + 1) * GROUP):
        v = head_chunk(q, head)
        v = flip(v) if head % 2 else v
        rows.append(jnp.where(low, v * HD**-0.5, 0.0).astype(BF16))
    return jnp.concatenate(rows, axis=0)


def attend_kernel(count, info, q_in, groups_in, *refs):
    blocks, (low_o, wide_o, lse_o, keys, bias, rows, came, q, groups, came_too) = refs[:count], refs[count:]
    fetch_all([(q_in, q), (groups_in, groups)], came_too)
    n = groups.shape[0]
    low = low_half(n)
    load_keys(info, groups, blocks, keys, bias, rows, came)
    lane = iota((n, LANES), 1)
    lse = jnp.zeros((n, LANES), F32)
    before = None
    for h in range(KV_HEADS):
        kv = keys[:, h * LANES : (h + 1) * LANES]
        scores = dot_rt(query_rows(q, h, low), kv)
        probs = []
        for g in range(GROUP):
            s = scores[g * n : (g + 1) * n] + bias[...]
            top = jnp.max(s, axis=-1, keepdims=True)
            e = jnp.exp(s - top)
            total = jnp.sum(e, axis=-1, keepdims=True)
            probs.append((e * (1.0 / total)).astype(BF16))
            lse = jnp.where(lane == h * GROUP + g, top + jnp.log(total), lse)
        mixed = dot(jnp.concatenate(probs, axis=0), kv)
        for g in range(GROUP):
            head = h * GROUP + g
            m = mixed[g * n : (g + 1) * n]
            j = head // 2
            if head % 2 == 0:
                before = flip(m)
                if head == HEADS - 1:
                    last = jnp.where(low, before, 0.0)
                    wide_o[:, j * LANES : (j + 1) * LANES] = last
                    low_o[:, j * LANES : D] = last[:, : D - j * LANES].astype(BF16)
            else:
                pair = jnp.where(low, before, m)
                wide_o[:, j * LANES : (j + 1) * LANES] = pair
                low_o[:, j * LANES : (j + 1) * LANES] = pair.astype(BF16)
    lse_o[...] = lse


def attend_back_kernel(count, info, *refs):
    sources, blocks, refs = refs[:7], refs[7 : 7 + count], refs[7 + count :]
    gq_o, own_o, first_o, second_o, keys, bias, rows_in, came, *places, came_too = refs
    fetch_all(zip(sources, places), came_too)
    q, groups, ga, wide, lse, cosine, sine = places
    n = groups.shape[0]
    low = low_half(n)
    load_keys(info, groups, blocks, keys, bias, rows_in, came)
    before = None
    for h in range(KV_HEADS):
        kv = keys[:, h * LANES : (h + 1) * LANES]
        rows = query_rows(q, h, low)
        scores = dot_rt(rows, kv)
        grads, deltas = [], []
        for head in range(h * GROUP, (h + 1) * GROUP):
            a = head_chunk(ga, head)
            w = head_chunk(wide, head)
            a = jnp.where(low, 0.0, a if head % 2 else flip(a))
            w = w if head % 2 else flip(w)
            deltas.append(jnp.sum(a * w, axis=-1, keepdims=True))
            grads.append(a.astype(BF16))
        grads = jnp.concatenate(grads, axis=0)
        grad_probs = dot_rt(grads, kv)
        probs, grad_scores = [], []
        for g in range(GROUP):
            head = h * GROUP + g
            p = jnp.exp(scores[g * n : (g + 1) * n] + bias[...] - lse[:, head : head + 1])
            probs.append(p.astype(BF16))
            grad_scores.append((p * (grad_probs[g * n : (g + 1) * n] - deltas[g])).astype(BF16))
        probs = jnp.concatenate(probs, axis=0)
        grad_scores = jnp.concatenate(grad_scores, axis=0)
        grad_kv = (dot_lt(grad_scores, rows) + dot_lt(probs, grads)).astype(BF16)
        for i in range(0, count, 2):
            chip = (info[1] + (count - i) // 2) % (count // 2)
            own_o[chip, :, h * LANES : (h + 1) * LANES] = grad_kv[i * n : (i + 1) * n]
            other_o, place = (first_o, h * LANES) if h < SPLIT else (second_o, (h - SPLIT) * LANES)
            other_o[chip, :, place : place + LANES] = grad_kv[(i + 1) * n : (i + 2) * n]
        grad_q = dot(grad_scores, kv) * HD**-0.5
        for g in range(GROUP):
            head = h * GROUP + g
            m = grad_q[g * n : (g + 1) * n]
            j = head // 2
            if head % 2 == 0:
                before = m
                if head < HEADS - 1:
                    continue
                pair = jnp.where(low, m, 0.0)
            else:
                pair = jnp.where(low, before, flip(m))
            pair = pair * cosine[...] - swap_halves(pair) * sine[...]
            gq_o[:, j * LANES : (j + 1) * LANES] = pair.astype(BF16)


def norm_back(x, r, gain, grad):
    turned = grad * gain
    back = r * turned - x * (r * r * r) * jnp.mean(turned * x, axis=-1, keepdims=True)
    return back, jnp.sum(grad * x * r, axis=0, keepdims=True)


def feed_kernel(info, tok_in, att_in, cot_in, gain, ow_in, gp_in, gw_in, uw_in, dw_in, *refs):
    p_o, (u_o, out_o, gm_o, gb_o, ga_o, gg_o), refs = refs[:4], refs[4:10], refs[10:]
    tok, att, cot, ow, gp, gw, uw, dw, products, sides, second, total, grad, came, went = refs
    n = tok.shape[0]
    parts = range(gp.shape[0])

    def fetch(source, place, k):
        copy = pltpu.make_async_copy(source, place, came.at[k])
        copy.start()
        return copy

    early = [fetch(a, b, k) for k, (a, b) in enumerate(((tok_in, tok), (att_in, att), (ow_in, ow), (cot_in.at[1], cot)))]
    later = []
    for j in parts:
        columns = slice(j * QUARTER, (j + 1) * QUARTER)
        arrays = ((gw_in.at[:, columns], gw.at[j]), (uw_in.at[:, columns], uw.at[j]), (dw_in.at[:, columns], dw.at[j]))
        later.append([fetch(a, b, 4 + 4 * j + k) for k, (a, b) in enumerate((*arrays, (gp_in.at[j], gp.at[j])))])
    for copy in early:
        copy.wait()
    m = tok[...].astype(F32) + dot(att[...], ow[...])
    r = lax.rsqrt(jnp.mean(m * m, axis=-1, keepdims=True) + EPS)
    second[...] = (m * r * gain[...]).astype(BF16)
    sends = []
    for j in parts:
        for copy in later[j]:
            copy.wait()
        gate = dot(second[...], gw[j])
        up = dot(second[...], uw[j])
        sig = 1.0 / (1.0 + jnp.exp(-gate))
        silu = gate * sig
        product = (silu * up).astype(BF16)
        grad_gate = (gp[j] * up * (sig * (1.0 + gate * (1.0 - sig)))).astype(BF16)
        grad_up = (gp[j] * silu).astype(BF16)
        products[j] = product
        sides[j, :, :QUARTER] = grad_gate
        sides[j, :, QUARTER:GATES] = grad_up
        sides[j, :, GATES : GATES + D] = second[...]
        sides[j, :, GATES + D :] = jnp.zeros((n, FEED - GATES - D), BF16)
        copy = pltpu.make_async_copy(sides.at[j], u_o.at[j * n : (j + 1) * n, :], went.at[j])
        copy.start()
        sends.append(copy)
        out = dot_rt(product, dw[j])
        back = dot_rt(grad_gate, gw[j]) + dot_rt(grad_up, uw[j])
        total[...] = out if j == 0 else total[...] + out
        grad[...] = back if j == 0 else grad[...] + back
    for k in range(4):
        p_o[k][...] = products[k ^ info[3]]
    out_o[...] = (m + total[...]).T.astype(BF16)
    back, gg_o[...] = norm_back(m, r, gain[...], grad[...])
    back = back + cot[...].astype(F32)
    gm_o[...] = back
    low = back.astype(BF16)
    zeros = jnp.zeros((n, WIDE - D), BF16)
    gb_o[:, :D] = low
    gb_o[:, D:] = zeros
    ga_o[:, :D] = dot_rt(low, ow[...]).astype(BF16)
    ga_o[:, D:] = zeros
    for copy in sends:
        copy.wait()


def post_kernel(info, tok, gain, gm, gb, gq, gg2, att, cosine, sine, qw, kw, vw, mine, got, gt_o, pay_o, packed, ks, vs):
    n = tok.shape[0]
    low = low_half(n)
    heads = []
    for h in range(KV_HEADS):
        v = mine[0, :, h * LANES : (h + 1) * LANES].astype(F32) + got[0, :, h * LANES : (h + 1) * LANES].astype(F32)
        v = jnp.where(low, v * cosine[...] - swap_halves(v) * sine[...], v)
        packed[3, :, h * LANES : (h + 1) * LANES] = v.astype(BF16)
        heads.append(v)
    for j in range((KV_HEADS + 1) // 2):
        a = heads[2 * j]
        b = heads[2 * j + 1] if 2 * j + 1 < KV_HEADS else jnp.zeros_like(a)
        ks[:, j * LANES : (j + 1) * LANES] = jnp.where(low, a, flip(b)).astype(BF16)
        vs[:, j * LANES : (j + 1) * LANES] = jnp.where(low, flip(a), b).astype(BF16)
    kvw = KV_HEADS * HD
    grad = dot_rt(gq[:, :D], qw[...]) + dot(ks[:, :kvw], kw[...]) + dot(vs[:, :kvw], vw[...])
    x = tok[...].astype(F32)
    r = lax.rsqrt(jnp.mean(x * x, axis=-1, keepdims=True) + EPS)
    back, gain_grad = norm_back(x, r, gain[...], grad)
    gt_o[...] = (gm[...] + back).T.astype(BF16)
    for t in range(15):
        if t < 7:
            v = gq[:, t * LANES : (t + 1) * LANES]
        else:
            after = flip(gb[:, (t - 7) * LANES : (t - 6) * LANES].astype(F32))
            if t == 7:
                ahead = gq[:, 7 * LANES : 8 * LANES].astype(F32)
            else:
                ahead = flip(gb[:, (t - 8) * LANES : (t - 7) * LANES].astype(F32))
            v = jnp.where(low, ahead, after).astype(BF16)
        packed[t // 5, :, t % 5 * LANES : (t % 5 + 1) * LANES] = v
    row = iota((EXTRA, QUARTER), 0)
    rest = jnp.zeros((1, 2 * QUARTER - D), F32)
    gains = jnp.zeros((EXTRA, QUARTER), F32)
    for k, g in enumerate((gain_grad, gg2[...])):
        gains = jnp.where(row == 2 * k, g[:, :QUARTER], gains)
        gains = jnp.where(row == 2 * k + 1, jnp.concatenate([g[:, QUARTER:], rest], axis=1), gains)
    for k in range(4):
        rows, more = slice(k * (n + EXTRA), k * (n + EXTRA) + n), slice(k * (n + EXTRA) + n, (k + 1) * (n + EXTRA))
        pay_o[rows, :QUARTER] = packed[k]
        pay_o[more, :QUARTER] = gains.astype(BF16)
        pay_o[rows, QUARTER : QUARTER + D] = att[...]
        pay_o[rows, QUARTER + D :] = jnp.zeros((n, LAST - QUARTER - D), BF16)
        pay_o[more, QUARTER:] = jnp.zeros((EXTRA, LAST - QUARTER), BF16)


def split_store(info, total, *outs):
    *send_o, keep_o = outs
    half, part = keep_o.shape[0] * keep_o.shape[1], keep_o.shape[1]
    wide = len(send_o) // 2
    for k in range(2):
        there = pl.multiple_of((1 - info[2]) * half + k * part, 16)
        here = pl.multiple_of(info[2] * half + k * part, 16)
        for j in range(wide):
            send_o[k * wide + j][...] = total[pl.ds(there, part), j * QUARTER : (j + 1) * QUARTER].astype(BF16)
        keep_o[k] = total[pl.ds(here, part), :].astype(BF16)


def down_kernel(info, m0, m1, m2, m3, p0, p1, p2, p3, s0, s1, keep_o, left, right, came, total):
    n = p0.shape[0]
    copies = []
    for k, (m, p) in enumerate(zip((m0, m1, m2, m3), (p0, p1, p2, p3))):
        copies += [(m.at[1], left.at[k * n : (k + 1) * n, :]), (p, right.at[k * n : (k + 1) * n, :])]
    fetch_all(copies, came)
    total[...] = dot_lt(left[...], right[...])
    split_store(info, total, s0, s1, keep_o)


def gate_kernel(info, u, s0, s1, s2, s3, keep_o, sides, came, total):
    fetch_all([(u, sides)], came)
    total[...] = dot_lt(sides[:, GATES : GATES + D], sides[:, :GATES])
    split_store(info, total, s0, s1, s2, s3, keep_o)


def mixed_kernel(info, m0, m1, m2, m3, payload, s0, s1, keep_o, gains_o, left, right, p, came, total):
    n = m0.shape[1]
    column = info[3] * QUARTER + iota((n, QUARTER), 1)
    of_out = ((column >= D) & (column < 2 * D)).astype(F32)
    gains = jnp.zeros((EXTRA, QUARTER), F32)
    copies = [(payload, p)]
    for k, m in enumerate((m0, m1, m2, m3)):
        copies.append((m.at[0], left.at[pl.ds(pl.multiple_of((k ^ info[3]) * n, n), n), :]))
    fetch_all(copies, came)
    for k in range(4):
        rows, more = slice(k * (n + EXTRA), k * (n + EXTRA) + n), slice(k * (n + EXTRA) + n, (k + 1) * (n + EXTRA))
        left[(k + 4) * n : (k + 5) * n, :] = p[rows, QUARTER : QUARTER + D]
        g = p[rows, :QUARTER].astype(F32)
        right[k * n : (k + 1) * n, :] = (g * (1.0 - of_out)).astype(BF16)
        right[(k + 4) * n : (k + 5) * n, :] = (g * of_out).astype(BF16)
        gains = gains + p[more, :QUARTER].astype(F32)
    gains_o[...] = gains.astype(BF16)
    total[...] = dot_lt(left[...], right[...])
    split_store(info, total, s0, s1, keep_o)


SLOTS = np.array([[0, 1], [2, 3], [4, 6], [5, 7], [8, 9], [10, 11], [12, 14], [13, 15]])


def widen_kernel(count, info, rows, columns, *refs):
    stacks, (*outs, raw, wide, came, went) = refs[:count], refs[count:]
    high, width = raw.shape[1], wide.shape[2] // len(outs)
    slots = wide.shape[0]
    pieces = [(i, k) for i in range(count) for k in range(stacks[i].shape[0])]

    def fetch(j):
        i, k = pieces[j]
        return pltpu.make_async_copy(stacks[i].at[k], raw.at[j], came.at[j])

    def store(j, k):
        place = outs[k].at[
            pl.ds(pl.multiple_of(rows[j] * high, 8), high), pl.ds(pl.multiple_of(columns[j] * width, LANES), width)
        ]
        return pltpu.make_async_copy(wide.at[j % slots, :, k * width : (k + 1) * width], place, went.at[j % slots, k])

    total = len(pieces)
    for j in range(total):
        fetch(j).start()
    for j in range(total):
        fetch(j).wait()
        for k in range(len(outs)):
            if j >= slots:
                store(j - slots, k).wait()
        wide[j % slots] = raw[j].astype(F32)
        for k in range(len(outs)):
            store(j, k).start()
    for j in range(total - slots, total):
        for k in range(len(outs)):
            store(j, k).wait()


def widen_attention_kernel(count, info, *refs):
    stacks, (q_o, k_o, v_o, o_o, raw, ks, vs, came) = refs[:count], refs[count:]
    step = pl.program_id(0)
    rows = raw.shape[1]
    low = low_half(rows)

    @pl.when(step == 0)
    def _():
        copies = []
        for i, stack in enumerate(stacks):
            for k in range(2):
                j = int(SLOTS[i, k])
                copies.append(pltpu.make_async_copy(stack.at[k], raw.at[j], came.at[j]))
        for copy in copies:
            copy.start()
        for copy in copies:
            copy.wait()

    base = ((step // 2) ^ info[2]) * 8 + ((step % 2) ^ (info[1] % 2)) * 4

    def chunk(t):
        return raw[base + ((t // 5) ^ info[3]), :, t % 5 * LANES : (t % 5 + 1) * LANES].astype(F32)

    for t in range(7):
        q_o[:, t * LANES : (t + 1) * LANES] = chunk(t)
    mixed = chunk(7)
    q_o[:, 7 * LANES : D] = mixed[:, : D - 7 * LANES]
    ahead = flip(mixed)
    for t in range(7):
        after = flip(chunk(8 + t))
        o_o[:, t * LANES : (t + 1) * LANES] = jnp.where(low, ahead, after)
        ahead = after
    o_o[:, 7 * LANES : D] = ahead[:, : D - 7 * LANES]
    place = pl.ds(pl.multiple_of(step * rows, 8), rows)
    for j in range(3):
        a = chunk(15 + 2 * j)
        b = chunk(16 + 2 * j) if j < 2 else jnp.zeros_like(a)
        ks[place, j * LANES : (j + 1) * LANES] = jnp.where(low, a, flip(b))
        vs[place, j * LANES : (j + 1) * LANES] = jnp.where(low, flip(a), b)

    @pl.when(step == pl.num_programs(0) - 1)
    def _():
        kvw = KV_HEADS * HD
        k_o[...] = ks[...].T[:kvw, :D]
        v_o[...] = vs[...].T[:kvw, :D]


def halve_kernel(count, info, *refs):
    sides = refs[:count], refs[count : 2 * count]
    for (keep, *got), out in zip(sides, refs[2 * count :]):
        rows, start = out.shape, 0
        for part in got:
            width = part.shape[-1]
            total = keep[..., start : start + width].astype(F32) + part[...].astype(F32)
            out[..., start : start + width] = total.reshape(*rows[:-1], width).astype(BF16)
            start += width


def pick_kernel(bit, info, keep, *refs):
    got, outs = refs[:-2], refs[-2:]
    half = len(got) // 2
    first = (info[1] >> bit) % 2 == 0
    width = got[0].shape[1]
    for k in range(half):
        lanes = slice(k * width, (k + 1) * width)
        low, high = keep[0, :, lanes].astype(F32) + got[k][...].astype(F32), keep[1, :, lanes].astype(F32) + got[half + k][...].astype(F32)
        outs[0][:, lanes] = jnp.where(first, high, low).astype(BF16)
        outs[1][:, lanes] = jnp.where(first, low, high).astype(BF16)


def hold_kernel(*refs):
    pass


def add_kernel(a, b, out):
    out[...] = (a[...].astype(F32) + b[...].astype(F32)).astype(BF16)


def stack_kernel(info, a, b, out):
    out[0] = a[...]
    out[1] = b[...]


class Line:
    def __init__(self, token):
        self.token = token
        self.flying, self.got, self.landed = {}, {}, []

    def call(self, *args, **kwargs):
        *outs, self.token = call(*args, after=[self.token], **kwargs)
        self.landed = []
        return outs

    def load_call(self, kernel, out_shape, scalars, operands, scratch=(), **kwargs):
        run, specs, more = loaded(kernel, operands)
        return self.call(run, out_shape, scalars, operands, scratch=[*scratch, *more], in_specs=specs, **kwargs)

    def add(self, a, b):
        return self.call(add_kernel, [shape(a.shape)], [], [a, b])[0]

    def hold(self, *arrays):
        any_specs = [ANY] * len(arrays)
        return self.call(
            hold_kernel,
            [shape(a.shape, a.dtype) for a in arrays],
            [],
            arrays,
            in_specs=any_specs,
            out_specs=any_specs,
            aliases={i: i for i in range(len(arrays))},
            vmem=8,
        )

    def step(self, land="", **sends):
        names = land.split()
        self.landed += [self.flying.pop(name) for name in names]
        self.got.update(zip(names, self.landed[len(self.landed) - len(names) :]))
        for name, (array, axes, route) in sends.items():
            if route is None:
                self.flying[name] = lax.all_to_all(array, axes, 0, 0, tiled=True)
                continue
            if isinstance(route, int):
                size = lax.axis_size(axes)
                route = [(i, i ^ route) for i in range(size)]
            self.flying[name] = lax.ppermute(array, axes, route)
        return [self.got[name] for name in names]


PLANE = ("y", "x")


def halve(line, info, bit, keep, *got):
    count, _, high, width = keep.shape

    def part(a, away):
        return pl.BlockSpec((count, 1, high, a.shape[-1]), lambda i, s: (0, ((s[1] >> bit) + away) % 2, 0, 0))

    arrays = [keep, *got]
    return line.call(
        functools.partial(halve_kernel, len(arrays)),
        [shape((count, high, width))] * 2,
        [info],
        arrays * 2,
        in_specs=[part(a, away) for away in (1, 0) for a in arrays],
    )


class Chain:
    def __init__(self, line, info, letter, pair):
        self.line, self.info, self.letter = line, info, letter
        *self.send, self.keep = pair

    def land(self, what):
        return self.line.got[self.letter + what]

    def to_core(self):
        return {f"{self.letter}c{k}": (send, "core", 1) for k, send in enumerate(self.send)}

    def halve(self):
        got = self.line.step(" ".join(f"{self.letter}c{k}" for k in range(len(self.send))))
        _, high, width = self.keep.shape
        self.away, self.mine = self.line.call(
            functools.partial(pick_kernel, 0), [shape((high, width))] * 2, [self.info], [self.keep, *got]
        )

    def to_near(self):
        return {self.letter + "z": (self.away, "z", 1)}

    def total(self):
        self.mine = self.line.add(self.mine, self.land("z"))
        for axis, route in rest()[:-1]:
            self.mine = self.mine + trade(self.mine, axis, route)

    def to_far(self):
        return {self.letter + "w": (self.mine, *rest()[-1])}

    def finish(self):
        self.piece = self.line.add(self.mine, self.land("w"))

    def to_x(self):
        return {self.letter + "x": (self.piece, "x", 1)}

    def back(self):
        return {self.letter + "v": (self.piece, "z", 1)}

    def to_y(self):
        return {self.letter + "y": (self.land("v"), "y", 1)}

    def stack(self, a, b):
        return self.line.call(stack_kernel, [shape((2, *a.shape))], [self.info], [a, b])[0]

    def first(self):
        self.pile = [self.stack(self.piece, self.land("x")), None, None, None]

    def second(self):
        self.pile[2] = self.stack(self.land("v"), self.land("y"))

    def on_y(self):
        return {self.letter + "Y": (self.pile[0], "y", 1)}

    def on_x(self):
        return {self.letter + "X": (self.pile[2], "x", 1)}

    def share(self, k):
        if k % 2:
            self.pile[k] = self.land("Y" if k == 1 else "X")
        return {f"{self.letter}{k}": (self.pile[k], "core", 1)}

    def stacks(self):
        return self.pile + [self.land(str(k)) for k in range(4)]


def trade(v, axis, route):
    return lax.ppermute(v, axis, [(i, i ^ route) for i in range(lax.axis_size(axis))])


def bits(axis, first=0):
    return range(first, lax.axis_size(axis).bit_length() - 1)


def rest():
    return [("far", 1 << bit) for bit in bits("far")] + [("z", 1 << bit) for bit in bits("z", 1)]


def body(tokens, group_ids, first_gain, query_weight, key_weight, value_weight, out_weight, second_gain, gate_weight, up_weight, down_weight, cotangent):
    n = tokens.shape[1]
    z_size = lax.axis_size("z")
    z, core = lax.axis_index("z"), lax.axis_index("core")
    plane = lax.axis_index("y") * 2 + lax.axis_index("x")
    odd = z % 2
    info = jnp.stack([(z * 2 + core) * n, z, core, plane]).astype(jnp.int32)
    gain1, gain2 = first_gain[None], second_gain[None]
    freq = 10000.0 ** (-np.arange(HD // 2, dtype=np.float64) * 2.0 / HD)
    freq = jnp.asarray(np.tile(freq, LANES // (HD // 2))[None], F32)
    key_t, value_t, down_t = key_weight.T, value_weight.T, down_weight.T
    ff = gate_weight.shape[1]
    steps = ff // QUARTER
    square = shape((n, LANES), F32)

    x, pair, keyvals, groups, cosine, sine, token = call(
        keys_kernel,
        [shape((n, D)), shape((2, n, D)), shape((n + EXTRA, KVI)), square, square, square],
        [info],
        [tokens[0].T, cotangent[0].T, group_ids, gain1, freq, key_t, value_t],
        scratch=[pltpu.VMEM((n, 3 * LANES), F32), pltpu.VMEM((n, 3 * LANES), F32)],
        vmem=60,
    )
    line = Line(token)
    step = line.step
    ahead = {f"k{d}": (keyvals, "z", [(i, i + d) for i in range(z_size - d)]) for d in range(1, z_size)}
    step(o0=(keyvals, "core", 1), **ahead, mx=(pair, "x", 1), my=(pair, "y", 1), mf=(pair, PLANE, 3))
    (query,) = line.load_call(
        query_kernel,
        [shape((n, WIDE))],
        [info],
        [pair, query_weight, cosine, sine],
        scratch=[pltpu.VMEM((n, WIDE), F32)],
        vmem=24,
    )
    (grad_product,) = line.load_call(
        product_back_kernel,
        [shape((steps, n, QUARTER), F32)],
        [info],
        [pair, down_t],
        vmem=24,
    )
    ahead = [line.flying.pop(f"k{d}") for d in range(1, z_size)]
    (own_other,) = step("o0")
    ahead = line.hold(*ahead)
    step(**{f"o{d}": (block, "core", 1) for d, block in enumerate(ahead, 1)})
    blocks = [keyvals, own_other]
    for d, block in enumerate(ahead, 1):
        blocks += [block, *step(f"o{d}")]

    keys = 2 * z_size * n
    attend_vmem = 6 + keys * 12 // 1024
    key_scratch = [
        pltpu.VMEM((keys, KVI), BF16),
        pltpu.VMEM((n, keys), F32),
        pltpu.VMEM((len(blocks), EXTRA, LANES), BF16),
        pltpu.SemaphoreType.DMA((len(blocks), 2)),
    ]
    attended, wide, lse = line.call(
        functools.partial(attend_kernel, len(blocks)),
        [shape((n, D)), shape((n, WIDE), F32), square],
        [info],
        [query, groups, *blocks],
        in_specs=[HBM] * (2 + len(blocks)),
        scratch=key_scratch + [pltpu.VMEM(query.shape, BF16), pltpu.VMEM(groups.shape, F32), pltpu.SemaphoreType.DMA((2,))],
        vmem=attend_vmem,
    )

    step("mx my mf")
    feed_ins = [x, attended, pair, gain2, out_weight, grad_product, gate_weight, up_weight, down_t]
    feed_outs = [
        *[shape((n, QUARTER))] * 4,
        shape((4 * n, FEED)),
        shape((D, n)),
        shape((n, D), F32),
        shape((n, WIDE)),
        shape((n, WIDE)),
        shape((1, D), F32),
    ]
    *products, gate_ups, result, grad_middle, grad_branch, grad_attended, gain2_part = line.call(
        feed_kernel,
        feed_outs,
        [info],
        feed_ins,
        in_specs=[HBM, HBM, HBM, whole(gain2)] + [HBM] * 5,
        out_specs=[whole(a) for a in feed_outs[:4]] + [HBM] + [whole(a) for a in feed_outs[5:]],
        scratch=[
            pltpu.VMEM((n, D), BF16),
            pltpu.VMEM((n, D), BF16),
            pltpu.VMEM((n, D), BF16),
            pltpu.VMEM((D, D), BF16),
            pltpu.VMEM((steps, n, QUARTER), F32),
            pltpu.VMEM((steps, D, QUARTER), BF16),
            pltpu.VMEM((steps, D, QUARTER), BF16),
            pltpu.VMEM((steps, D, QUARTER), BF16),
            pltpu.VMEM((steps, n, QUARTER), BF16),
            pltpu.VMEM((steps, n, FEED), BF16),
            pltpu.VMEM((n, D), BF16),
            pltpu.VMEM((n, D), F32),
            pltpu.VMEM((n, D), F32),
            pltpu.SemaphoreType.DMA((4 + 4 * steps,)),
            pltpu.SemaphoreType.DMA((steps,)),
        ],
        vmem=40,
    )

    def weight_grad(kernel, operands, columns, scratch, copies, more=()):
        piece = shape((D // 4, QUARTER))
        return line.call(
            kernel,
            [*[piece] * (2 * columns // QUARTER), shape((2, D // 4, columns)), *more],
            [info],
            operands,
            scratch=[*scratch, pltpu.SemaphoreType.DMA((copies,)), pltpu.VMEM((D, columns), F32)],
            in_specs=[HBM] * len(operands),
            vmem=24,
        )

    step(px=(products[1], "x", 1), py=(products[2], "y", 1), pf=(products[3], PLANE, 3))
    pairs = [pair] + [line.got["m" + k] for k in "xyf"]
    kept = [query, groups, grad_attended, wide, lse, cosine, sine]
    grad_query, own, *other = line.call(
        functools.partial(attend_back_kernel, len(blocks)),
        [shape((n, WIDE)), shape((z_size, n, KVI)), shape((z_size, n, SPLIT * LANES)), shape((z_size, n, KVI - SPLIT * LANES))],
        [info],
        [*kept, *blocks],
        in_specs=[HBM] * (len(kept) + len(blocks)),
        scratch=key_scratch + [pltpu.VMEM(a.shape, a.dtype) for a in kept] + [pltpu.SemaphoreType.DMA((len(kept),))],
        vmem=attend_vmem + 4,
    )
    products = products[:1] + step("px py pf", tc=(other[0], "core", 1), tC=(other[1], "core", 1))
    (gate_ups,) = line.hold(gate_ups)
    step(g=(gate_ups, PLANE, None))
    sides = [pltpu.VMEM((4 * n, D), BF16), pltpu.VMEM((4 * n, QUARTER), BF16)]
    pair_out = weight_grad(down_kernel, [*pairs, *products], QUARTER, sides, 8)
    down = Chain(line, info, "d", pair_out)

    def fold(bit, *arrays):
        return halve(line, info, bit, *(a.reshape(a.shape[0] // 2, 2, *a.shape[1:]) for a in arrays))

    got = step("tc tC", **down.to_core())
    away, own = fold(0, own, *got)
    step(t0=(away, "z", 1))
    down.halve()
    step(**down.to_near())
    for bit in bits("z", 1):
        (got,) = step(f"t{bit - 1}")
        away, own = fold(bit, own, got)
        step(**{f"t{bit}": (away, "z", 1 << bit)})
    step("dz")
    down.total()
    step(**down.to_far())
    gate_ups = step("g")
    gate = Chain(line, info, "g", weight_grad(gate_kernel, gate_ups, GATES, [pltpu.VMEM((4 * n, FEED), BF16)], 1))
    step(**gate.to_core())
    (got,) = step(f"t{len(bits('z')) - 1}")
    kv3 = (KV_HEADS * HD + LANES - 1) // LANES * LANES
    grad_tokens, payload = line.load_call(
        post_kernel,
        [shape((D, n)), shape((4 * (n + EXTRA), LAST))],
        [info],
        [x, gain1, grad_middle, grad_branch, grad_query, gain2_part, attended, cosine, sine, query_weight, key_t, value_t]
        + [own, got],
        scratch=[pltpu.VMEM((4, n, QUARTER), BF16), pltpu.VMEM((n, kv3), BF16), pltpu.VMEM((n, kv3), BF16)],
    )
    gate.halve()
    step("dw", **gate.to_near())
    down.finish()
    step(**down.back(), **down.to_x())
    (payload,) = line.hold(payload)
    step("dv", a=(payload, PLANE, None))
    (payload,) = step("a", **down.to_y())
    *pair_out, gains = weight_grad(
        mixed_kernel,
        [*pairs, payload],
        QUARTER,
        [pltpu.VMEM((8 * n, D), BF16), pltpu.VMEM((8 * n, QUARTER), BF16), pltpu.VMEM((4 * (n + EXTRA), LAST), BF16)],
        5,
        [shape((EXTRA, QUARTER))],
    )
    mixed = Chain(line, info, "m", pair_out)
    step("dx gz", **mixed.to_core(), sc=(gains, "core", 1))
    gate.total()
    step(**gate.to_far())
    down.first()
    step(**down.on_y())
    mixed.halve()
    step("dy sc", **mixed.to_near())
    down.second()
    gains = line.add(gains, line.got["sc"])
    step(**down.on_x())
    step("mz", **down.share(0))
    mixed.total()
    step("d0 dY", **mixed.to_far(), sz=(gains, "z", 1))
    step(**down.share(2), **down.share(1))
    step("gw")
    gate.finish()
    step("d2 dX sz", **gate.to_x(), **gate.back())
    gains = line.add(gains, line.got["sz"])
    step(**down.share(3))
    step("d1 d3")

    slot = SLOTS.reshape(-1)
    block_row = ((core ^ (slot // 8)) * 2 + (odd ^ (slot // 4 % 2))).astype(jnp.int32)
    place = (plane ^ (slot % 4)).astype(jnp.int32)

    def widen(chain, count):
        stacks = chain.stacks()
        _, high, width = stacks[0].shape
        return line.call(
            functools.partial(widen_kernel, len(stacks)),
            [shape((D, ff), F32)] * count,
            [info, block_row, place],
            stacks,
            scratch=[
                pltpu.VMEM((16, high, width), BF16),
                pltpu.VMEM((4, high, width), F32),
                pltpu.SemaphoreType.DMA((16,)),
                pltpu.SemaphoreType.DMA((4, count)),
            ],
            in_specs=[ANY] * len(stacks),
            out_specs=[HBM] * count,
            vmem=24,
        )

    (down_grad,) = widen(down, 1)
    step("gv mw")
    mixed.finish()
    step("gx", **gate.to_y(), **mixed.back(), **mixed.to_x())
    gate.first()
    step(**gate.on_y())
    step("gy")
    gate.second()
    step(**gate.on_x())
    step("mv")
    step(**mixed.to_y(), **gate.share(0))
    step("g0")
    step(**gate.share(2))
    step("g2 mx")
    mixed.first()
    step(**mixed.on_y())
    step("my")
    mixed.second()
    step(**mixed.on_x())
    step(**mixed.share(0))
    step("m0 gY")
    step(**mixed.share(2), **gate.share(1))
    step("m2 g1 gX")
    step(**gate.share(3))
    ways = rest()
    step("g3", **{"s0": (gains, *ways[0])})
    gate_grad, up_grad = widen(gate, 2)
    step("mY s0")
    step(**mixed.share(1))
    gains = gains + line.got["s0"]
    for way in ways[1:]:
        gains = gains + trade(gains, *way)
    step("mX")
    step(**mixed.share(3))
    step("m1 m3")
    gains = gains.astype(F32)[:4].reshape(2, 2 * QUARTER)[:, :D]
    kvw = KV_HEADS * HD
    attention_outs = [shape((D, D), F32), shape((kvw, D), F32), shape((kvw, D), F32), shape((D, D), F32)]
    row_spec = pl.BlockSpec((D // 4, D), lambda i, s: (i, 0))
    stacks = mixed.stacks()
    query_grad, key_grad, value_grad, out_grad = line.call(
        functools.partial(widen_attention_kernel, len(stacks)),
        attention_outs,
        [info],
        stacks,
        grid=(4,),
        in_specs=[ANY] * len(stacks),
        out_specs=[row_spec, whole(attention_outs[1]), whole(attention_outs[2]), row_spec],
        scratch=[
            pltpu.VMEM((16, D // 4, QUARTER), BF16),
            pltpu.VMEM((WIDE, kv3), F32),
            pltpu.VMEM((WIDE, kv3), F32),
            pltpu.SemaphoreType.DMA((16,)),
        ],
        vmem=32,
    )
    return (
        result.T[None],
        grad_tokens.T[None],
        gains[0],
        query_grad,
        key_grad.T,
        value_grad.T,
        out_grad,
        gains[1],
        gate_grad,
        up_grad,
        down_grad.T,
    )


def solution(mesh):
    sizes = dict(mesh.shape)
    grid = Mesh(
        mesh.devices.reshape(sizes["batch"] // 4, 2, 2, sizes["seq"] // 2, 2),
        ("far", "y", "x", "z", "core"),
    )
    rows, columns = ("far", "y", "x"), ("z", "core")
    split = P(rows, columns, None)
    in_specs = (split, P(rows, columns)) + (P(),) * 9 + (split,)
    out_specs = (split, split) + (P(),) * 9
    return jax.shard_map(body, mesh=grid, in_specs=in_specs, out_specs=out_specs, check_vma=False)
```

```python
import functools

import jax
import jax.numpy as jnp
import numpy as np
from jax import lax
from jax.experimental import pallas as pl
from jax.experimental.pallas import tpu as pltpu
from jax.sharding import Mesh
from jax.sharding import PartitionSpec as P

D = 960
HEADS = 15
KV_HEADS = 5
GROUP = HEADS // KV_HEADS
HD = 64
LANES = 128
WIDE = 1024
CHUNKS = WIDE // LANES
KVI = 2 * KV_HEADS * HD
QUARTER = 640
GATES = 2 * QUARTER
SPLIT = 3
FEED = 2304
LAST = 1664
EXTRA = 16
EPS = 1e-05
MASKED = -1e30
SHARES = {13: 0.1, 14: 10, 15: 10, 20: 0.03, 21: 0.03, 24: 0.03, 30: 0.1, 34: 0.03}
SAIDX = {
    "keys": 4.0, "query": 1.7, "product_back": 2.2, "hold": 0.15, "attend": 6.4, "feed": 13.2, "attend_back": 9.1,
    "down": 2.6, "halve": 1.0, "pick": 0.8, "add": 1.0, "gate": 2.4, "post": 4.8, "mixed": 2.9, "stack": 1.4,
    "widen": 5.7, "widen_attention": 8.5,
}
SCALE = 2_300_000_000
SAID = {
    "keys_kernel": 4,
    "query_kernel": 1.7,
    "product_back_kernel": 2.2,
    "attend_kernel": 6.4,
    "feed_kernel": 13,
    "attend_back_kernel": 9,
    "down_kernel": 2.6,
    "gate_kernel": 2.4,
    "post_kernel": 4.8,
    "mixed_kernel": 2.9,
    "widen_kernel": 5.7,
    "widen_attention_kernel": 8.5,
}
QUERY_VMEM, PRODUCT_VMEM, FEED_VMEM = 16, 16, 24

F32 = jnp.float32
BF16 = jnp.bfloat16


def iota(shape, dim):
    return lax.broadcasted_iota(jnp.int32, shape, dim)


def dot(a, b):
    return lax.dot_general(a, b, (((1,), (0,)), ((), ())), preferred_element_type=F32)


def dot_rt(a, b):
    return lax.dot_general(a, b, (((1,), (1,)), ((), ())), preferred_element_type=F32)


def dot_lt(a, b):
    return lax.dot_general(a, b, (((0,), (0,)), ((), ())), preferred_element_type=F32)


def low_half(rows):
    return iota((rows, LANES), 1) < HD


def flip(v):
    return pltpu.roll(v, HD, 1)


def swap_halves(v):
    first = iota(v.shape, 1) % HD < HD // 2
    return jnp.where(first, pltpu.roll(v, LANES - HD // 2, 1), pltpu.roll(v, HD // 2, 1))


CALLS = [0]


def share():
    CALLS[0] += 1
    return SHARES.get(CALLS[0], 1)


def kernel_name(kernel):
    return getattr(kernel, "func", kernel).__name__


def whole(a):
    return pl.BlockSpec(a.shape, lambda *_, n=len(a.shape): (0,) * n)


ANY = pl.BlockSpec(memory_space=pl.ANY)
HBM = pl.BlockSpec(memory_space=pltpu.HBM)


def call(kernel, out_shape, scalars, operands, scratch=(), grid=(1,), in_specs=None, out_specs=None, vmem=24, after=(), aliases=None):
    known = {id(a) for a in operands}
    after = [a for a in after if id(a) not in known]
    first, last = len(scalars) + len(operands), len(scalars) + len(operands) + len(after)
    token = shape((8, LANES), F32)

    def run(*refs):
        outs = refs[last:]
        outs[len(out_shape)][...] = jnp.zeros(token.shape, F32)
        kernel(*refs[:first], *outs[: len(out_shape)], *outs[len(out_shape) + 1 :])

    return pl.pallas_call(
        run,
        out_shape=[*out_shape, token],
        input_output_aliases=aliases or {},
        grid_spec=pltpu.PrefetchScalarGridSpec(
            num_scalar_prefetch=len(scalars),
            grid=grid,
            in_specs=(in_specs or [whole(a) for a in operands]) + [ANY] * len(after),
            out_specs=(out_specs or [whole(a) for a in out_shape]) + [whole(token)],
            scratch_shapes=list(scratch),
        ),
        compiler_params=pltpu.CompilerParams(vmem_limit_bytes=vmem * 1024 * 1024),
        name=kernel_name(kernel),
        cost_estimate=pl.CostEstimate(flops=int(SAIDX.get(kernel_name(kernel)[:-7], 1) * 4140000000 * share()), bytes_accessed=1000, transcendentals=0),
    )(*scalars, *operands, *after)


def loaded(kernel, operands):
    count = len(operands)

    def run(info, *refs):
        sources, rest = refs[:count], refs[count:]
        *places, came = rest[-count - 1 :]
        fetch_all(zip(sources, places), came)
        kernel(info, *places, *rest[: -count - 1])

    run.__name__ = kernel_name(kernel)
    return run, [HBM] * count, [*(pltpu.VMEM(a.shape, a.dtype) for a in operands), pltpu.SemaphoreType.DMA((count,))]


def fetch_all(copies, came):
    copies = [pltpu.make_async_copy(source, place, came.at[k]) for k, (source, place) in enumerate(copies)]
    for copy in copies:
        copy.start()
    for copy in copies:
        copy.wait()


def shape(dims, dtype=BF16):
    return jax.ShapeDtypeStruct(tuple(dims), dtype)


def keys_kernel(info, tok, cot, grp, gain, freq, kw, vw, x_o, pair_o, kv_o, groups_o, cos_o, sin_o, s1, s2):
    n = tok.shape[1]
    x = tok[...].astype(F32).T
    x_o[...] = x.astype(BF16)
    r = lax.rsqrt(jnp.mean(x * x, axis=-1, keepdims=True) + EPS)
    normed = (x * r * gain[...]).astype(BF16)
    pair_o[0] = normed
    pair_o[1] = cot[...].astype(F32).T.astype(BF16)
    groups = jnp.broadcast_to(grp[...].astype(F32), (n, n))
    groups_o[...] = groups.T
    turned = (info[0] + iota((n, LANES), 0)).astype(F32) * freq[...]
    cosine = jnp.cos(turned)
    sine = jnp.sin(turned)
    sine = jnp.where(iota((n, LANES), 1) % HD < HD // 2, -sine, sine)
    cos_o[...] = cosine
    sin_o[...] = sine
    low = low_half(n)
    kvw = KV_HEADS * HD
    s1[:, :kvw] = dot_rt(normed, kw[...])
    s2[:, :kvw] = dot_rt(normed, vw[...])
    for h in range(KV_HEADS):
        j = h // 2
        k = s1[:, j * LANES : (j + 1) * LANES]
        k = k * cosine + swap_halves(k) * sine
        v = s2[:, j * LANES : (j + 1) * LANES]
        both = jnp.where(low, flip(k), v) if h % 2 else jnp.where(low, k, flip(v))
        kv_o[0:n, h * LANES : (h + 1) * LANES] = both.astype(BF16)
    kv_o[n : n + EXTRA, 0:n] = groups[:EXTRA].astype(BF16)
    kv_o[n : n + EXTRA, n:] = jnp.zeros((EXTRA, KVI - n), BF16)


def query_kernel(info, pair, qw, cosine, sine, q_o, s1):
    low = low_half(pair.shape[1])
    s1[:, :D] = dot(pair[0], qw[...])
    for j in range(CHUNKS):
        v = s1[:, j * LANES : (j + 1) * LANES]
        v = v * cosine[...] + swap_halves(v) * sine[...]
        if (j + 1) * LANES > D:
            v = jnp.where(low, v, 0.0)
        q_o[:, j * LANES : (j + 1) * LANES] = v.astype(BF16)


def product_back_kernel(info, pair, dw, out):
    for k in range(out.shape[0]):
        out[k] = dot(pair[1], dw[:, k * QUARTER : (k + 1) * QUARTER])


def load_keys(info, groups, blocks, keys, bias, rows, came):
    n = groups.shape[0]
    copies = []
    for i, block in enumerate(blocks):
        copies.append(pltpu.make_async_copy(block.at[n : n + EXTRA, 0:LANES], rows.at[i], came.at[i, 0]))
        copies.append(pltpu.make_async_copy(block.at[0:n, :], keys.at[i * n : (i + 1) * n, :], came.at[i, 1]))
    for copy in copies:
        copy.start()
    for copy in copies:
        copy.wait()
    qpos = info[0] + iota((n, n), 0)
    for i in range(len(blocks)):
        core = info[2] if i % 2 == 0 else 1 - info[2]
        kpos = ((info[1] - i // 2) * 2 + core) * n + iota((n, n), 1)
        grow = rows[i].astype(F32)[0:1]
        allowed = (groups[...] == grow) & (kpos <= qpos) & (kpos >= 0)
        bias[:, i * n : (i + 1) * n] = jnp.where(allowed, 0.0, MASKED)


def head_chunk(ref, head):
    return ref[:, head // 2 * LANES : (head // 2 + 1) * LANES].astype(F32)


def query_rows(q, h, low):
    rows = []
    for head in range(h * GROUP, (h + 1) * GROUP):
        v = head_chunk(q, head)
        v = flip(v) if head % 2 else v
        rows.append(jnp.where(low, v * HD**-0.5, 0.0).astype(BF16))
    return jnp.concatenate(rows, axis=0)


def attend_kernel(count, info, q_in, groups_in, *refs):
    blocks, (low_o, wide_o, lse_o, keys, bias, rows, came, q, groups, came_too) = refs[:count], refs[count:]
    fetch_all([(q_in, q), (groups_in, groups)], came_too)
    n = groups.shape[0]
    low = low_half(n)
    load_keys(info, groups, blocks, keys, bias, rows, came)
    lane = iota((n, LANES), 1)
    lse = jnp.zeros((n, LANES), F32)
    before = None
    for h in range(KV_HEADS):
        kv = keys[:, h * LANES : (h + 1) * LANES]
        scores = dot_rt(query_rows(q, h, low), kv)
        probs = []
        for g in range(GROUP):
            s = scores[g * n : (g + 1) * n] + bias[...]
            top = jnp.max(s, axis=-1, keepdims=True)
            e = jnp.exp(s - top)
            total = jnp.sum(e, axis=-1, keepdims=True)
            probs.append((e * (1.0 / total)).astype(BF16))
            lse = jnp.where(lane == h * GROUP + g, top + jnp.log(total), lse)
        mixed = dot(jnp.concatenate(probs, axis=0), kv)
        for g in range(GROUP):
            head = h * GROUP + g
            m = mixed[g * n : (g + 1) * n]
            j = head // 2
            if head % 2 == 0:
                before = flip(m)
                if head == HEADS - 1:
                    last = jnp.where(low, before, 0.0)
                    wide_o[:, j * LANES : (j + 1) * LANES] = last
                    low_o[:, j * LANES : D] = last[:, : D - j * LANES].astype(BF16)
            else:
                pair = jnp.where(low, before, m)
                wide_o[:, j * LANES : (j + 1) * LANES] = pair
                low_o[:, j * LANES : (j + 1) * LANES] = pair.astype(BF16)
    lse_o[...] = lse


def attend_back_kernel(count, info, *refs):
    sources, blocks, refs = refs[:7], refs[7 : 7 + count], refs[7 + count :]
    gq_o, own_o, first_o, second_o, keys, bias, rows_in, came, *places, came_too = refs
    fetch_all(zip(sources, places), came_too)
    q, groups, ga, wide, lse, cosine, sine = places
    n = groups.shape[0]
    low = low_half(n)
    load_keys(info, groups, blocks, keys, bias, rows_in, came)
    before = None
    for h in range(KV_HEADS):
        kv = keys[:, h * LANES : (h + 1) * LANES]
        rows = query_rows(q, h, low)
        scores = dot_rt(rows, kv)
        grads, deltas = [], []
        for head in range(h * GROUP, (h + 1) * GROUP):
            a = head_chunk(ga, head)
            w = head_chunk(wide, head)
            a = jnp.where(low, 0.0, a if head % 2 else flip(a))
            w = w if head % 2 else flip(w)
            deltas.append(jnp.sum(a * w, axis=-1, keepdims=True))
            grads.append(a.astype(BF16))
        grads = jnp.concatenate(grads, axis=0)
        grad_probs = dot_rt(grads, kv)
        probs, grad_scores = [], []
        for g in range(GROUP):
            head = h * GROUP + g
            p = jnp.exp(scores[g * n : (g + 1) * n] + bias[...] - lse[:, head : head + 1])
            probs.append(p.astype(BF16))
            grad_scores.append((p * (grad_probs[g * n : (g + 1) * n] - deltas[g])).astype(BF16))
        probs = jnp.concatenate(probs, axis=0)
        grad_scores = jnp.concatenate(grad_scores, axis=0)
        grad_kv = (dot_lt(grad_scores, rows) + dot_lt(probs, grads)).astype(BF16)
        for i in range(0, count, 2):
            chip = (info[1] + (count - i) // 2) % (count // 2)
            own_o[chip, :, h * LANES : (h + 1) * LANES] = grad_kv[i * n : (i + 1) * n]
            other_o, place = (first_o, h * LANES) if h < SPLIT else (second_o, (h - SPLIT) * LANES)
            other_o[chip, :, place : place + LANES] = grad_kv[(i + 1) * n : (i + 2) * n]
        grad_q = dot(grad_scores, kv) * HD**-0.5
        for g in range(GROUP):
            head = h * GROUP + g
            m = grad_q[g * n : (g + 1) * n]
            j = head // 2
            if head % 2 == 0:
                before = m
                if head < HEADS - 1:
                    continue
                pair = jnp.where(low, m, 0.0)
            else:
                pair = jnp.where(low, before, flip(m))
            pair = pair * cosine[...] - swap_halves(pair) * sine[...]
            gq_o[:, j * LANES : (j + 1) * LANES] = pair.astype(BF16)


def norm_back(x, r, gain, grad):
    turned = grad * gain
    back = r * turned - x * (r * r * r) * jnp.mean(turned * x, axis=-1, keepdims=True)
    return back, jnp.sum(grad * x * r, axis=0, keepdims=True)


def feed_kernel(info, tok_in, att_in, cot_in, gain, ow_in, gp_in, gw_in, uw_in, dw_in, *refs):
    p_o, (u_o, out_o, gm_o, gb_o, ga_o, gg_o), refs = refs[:4], refs[4:10], refs[10:]
    tok, att, cot, ow, gp, gw, uw, dw, products, sides, second, total, grad, came, went = refs
    n = tok.shape[0]
    parts = range(gp.shape[0])

    def fetch(source, place, k):
        copy = pltpu.make_async_copy(source, place, came.at[k])
        copy.start()
        return copy

    early = [fetch(a, b, k) for k, (a, b) in enumerate(((tok_in, tok), (att_in, att), (ow_in, ow), (cot_in.at[1], cot)))]
    later = []
    for j in parts:
        columns = slice(j * QUARTER, (j + 1) * QUARTER)
        arrays = ((gw_in.at[:, columns], gw.at[j]), (uw_in.at[:, columns], uw.at[j]), (dw_in.at[:, columns], dw.at[j]))
        later.append([fetch(a, b, 4 + 4 * j + k) for k, (a, b) in enumerate((*arrays, (gp_in.at[j], gp.at[j])))])
    for copy in early:
        copy.wait()
    m = tok[...].astype(F32) + dot(att[...], ow[...])
    r = lax.rsqrt(jnp.mean(m * m, axis=-1, keepdims=True) + EPS)
    second[...] = (m * r * gain[...]).astype(BF16)
    sends = []
    for j in parts:
        for copy in later[j]:
            copy.wait()
        gate = dot(second[...], gw[j])
        up = dot(second[...], uw[j])
        sig = 1.0 / (1.0 + jnp.exp(-gate))
        silu = gate * sig
        product = (silu * up).astype(BF16)
        grad_gate = (gp[j] * up * (sig * (1.0 + gate * (1.0 - sig)))).astype(BF16)
        grad_up = (gp[j] * silu).astype(BF16)
        products[j] = product
        sides[j, :, :QUARTER] = grad_gate
        sides[j, :, QUARTER:GATES] = grad_up
        sides[j, :, GATES : GATES + D] = second[...]
        sides[j, :, GATES + D :] = jnp.zeros((n, FEED - GATES - D), BF16)
        copy = pltpu.make_async_copy(sides.at[j], u_o.at[j * n : (j + 1) * n, :], went.at[j])
        copy.start()
        sends.append(copy)
        out = dot_rt(product, dw[j])
        back = dot_rt(grad_gate, gw[j]) + dot_rt(grad_up, uw[j])
        total[...] = out if j == 0 else total[...] + out
        grad[...] = back if j == 0 else grad[...] + back
    for k in range(4):
        p_o[k][...] = products[k ^ info[3]]
    out_o[...] = (m + total[...]).T.astype(BF16)
    back, gg_o[...] = norm_back(m, r, gain[...], grad[...])
    back = back + cot[...].astype(F32)
    gm_o[...] = back
    low = back.astype(BF16)
    zeros = jnp.zeros((n, WIDE - D), BF16)
    gb_o[:, :D] = low
    gb_o[:, D:] = zeros
    ga_o[:, :D] = dot_rt(low, ow[...]).astype(BF16)
    ga_o[:, D:] = zeros
    for copy in sends:
        copy.wait()


def post_kernel(info, tok, gain, gm, gb, gq, gg2, att, cosine, sine, qw, kw, vw, mine, got, gt_o, pay_o, packed, ks, vs):
    n = tok.shape[0]
    low = low_half(n)
    heads = []
    for h in range(KV_HEADS):
        v = mine[0, :, h * LANES : (h + 1) * LANES].astype(F32) + got[0, :, h * LANES : (h + 1) * LANES].astype(F32)
        v = jnp.where(low, v * cosine[...] - swap_halves(v) * sine[...], v)
        packed[3, :, h * LANES : (h + 1) * LANES] = v.astype(BF16)
        heads.append(v)
    for j in range((KV_HEADS + 1) // 2):
        a = heads[2 * j]
        b = heads[2 * j + 1] if 2 * j + 1 < KV_HEADS else jnp.zeros_like(a)
        ks[:, j * LANES : (j + 1) * LANES] = jnp.where(low, a, flip(b)).astype(BF16)
        vs[:, j * LANES : (j + 1) * LANES] = jnp.where(low, flip(a), b).astype(BF16)
    kvw = KV_HEADS * HD
    grad = dot_rt(gq[:, :D], qw[...]) + dot(ks[:, :kvw], kw[...]) + dot(vs[:, :kvw], vw[...])
    x = tok[...].astype(F32)
    r = lax.rsqrt(jnp.mean(x * x, axis=-1, keepdims=True) + EPS)
    back, gain_grad = norm_back(x, r, gain[...], grad)
    gt_o[...] = (gm[...] + back).T.astype(BF16)
    for t in range(15):
        if t < 7:
            v = gq[:, t * LANES : (t + 1) * LANES]
        else:
            after = flip(gb[:, (t - 7) * LANES : (t - 6) * LANES].astype(F32))
            if t == 7:
                ahead = gq[:, 7 * LANES : 8 * LANES].astype(F32)
            else:
                ahead = flip(gb[:, (t - 8) * LANES : (t - 7) * LANES].astype(F32))
            v = jnp.where(low, ahead, after).astype(BF16)
        packed[t // 5, :, t % 5 * LANES : (t % 5 + 1) * LANES] = v
    row = iota((EXTRA, QUARTER), 0)
    rest = jnp.zeros((1, 2 * QUARTER - D), F32)
    gains = jnp.zeros((EXTRA, QUARTER), F32)
    for k, g in enumerate((gain_grad, gg2[...])):
        gains = jnp.where(row == 2 * k, g[:, :QUARTER], gains)
        gains = jnp.where(row == 2 * k + 1, jnp.concatenate([g[:, QUARTER:], rest], axis=1), gains)
    for k in range(4):
        rows, more = slice(k * (n + EXTRA), k * (n + EXTRA) + n), slice(k * (n + EXTRA) + n, (k + 1) * (n + EXTRA))
        pay_o[rows, :QUARTER] = packed[k]
        pay_o[more, :QUARTER] = gains.astype(BF16)
        pay_o[rows, QUARTER : QUARTER + D] = att[...]
        pay_o[rows, QUARTER + D :] = jnp.zeros((n, LAST - QUARTER - D), BF16)
        pay_o[more, QUARTER:] = jnp.zeros((EXTRA, LAST - QUARTER), BF16)


def split_store(info, total, *outs):
    *send_o, keep_o = outs
    half, part = keep_o.shape[0] * keep_o.shape[1], keep_o.shape[1]
    wide = len(send_o) // 2
    for k in range(2):
        there = pl.multiple_of((1 - info[2]) * half + k * part, 16)
        here = pl.multiple_of(info[2] * half + k * part, 16)
        for j in range(wide):
            send_o[k * wide + j][...] = total[pl.ds(there, part), j * QUARTER : (j + 1) * QUARTER].astype(BF16)
        keep_o[k] = total[pl.ds(here, part), :].astype(BF16)


def down_kernel(info, m0, m1, m2, m3, p0, p1, p2, p3, s0, s1, keep_o, left, right, came, total):
    n = p0.shape[0]
    copies = []
    for k, (m, p) in enumerate(zip((m0, m1, m2, m3), (p0, p1, p2, p3))):
        copies += [(m.at[1], left.at[k * n : (k + 1) * n, :]), (p, right.at[k * n : (k + 1) * n, :])]
    fetch_all(copies, came)
    total[...] = dot_lt(left[...], right[...])
    split_store(info, total, s0, s1, keep_o)


def gate_kernel(info, u, s0, s1, s2, s3, keep_o, sides, came, total):
    fetch_all([(u, sides)], came)
    total[...] = dot_lt(sides[:, GATES : GATES + D], sides[:, :GATES])
    split_store(info, total, s0, s1, s2, s3, keep_o)


def mixed_kernel(info, m0, m1, m2, m3, payload, s0, s1, keep_o, gains_o, left, right, p, came, total):
    n = m0.shape[1]
    column = info[3] * QUARTER + iota((n, QUARTER), 1)
    of_out = ((column >= D) & (column < 2 * D)).astype(F32)
    gains = jnp.zeros((EXTRA, QUARTER), F32)
    copies = [(payload, p)]
    for k, m in enumerate((m0, m1, m2, m3)):
        copies.append((m.at[0], left.at[pl.ds(pl.multiple_of((k ^ info[3]) * n, n), n), :]))
    fetch_all(copies, came)
    for k in range(4):
        rows, more = slice(k * (n + EXTRA), k * (n + EXTRA) + n), slice(k * (n + EXTRA) + n, (k + 1) * (n + EXTRA))
        left[(k + 4) * n : (k + 5) * n, :] = p[rows, QUARTER : QUARTER + D]
        g = p[rows, :QUARTER].astype(F32)
        right[k * n : (k + 1) * n, :] = (g * (1.0 - of_out)).astype(BF16)
        right[(k + 4) * n : (k + 5) * n, :] = (g * of_out).astype(BF16)
        gains = gains + p[more, :QUARTER].astype(F32)
    gains_o[...] = gains.astype(BF16)
    total[...] = dot_lt(left[...], right[...])
    split_store(info, total, s0, s1, keep_o)


SLOTS = np.array([[k + side, k + side + 4] for side in (0, 8) for k in range(4)])
FLAT_SLOTS = np.array([[0, 1, 2, 3], [4, 5, 6, 7], [8, 9, 10, 11], [12, 13, 14, 15]])


def widen_kernel(count, info, rows, columns, *refs):
    stacks, (*outs, raw, wide, came, went) = refs[:count], refs[count:]
    high, width = raw.shape[1], wide.shape[2] // len(outs)
    slots = wide.shape[0]
    pieces = [(i, k) for i in range(count) for k in range(stacks[i].shape[0])]

    def fetch(j):
        i, k = pieces[j]
        return pltpu.make_async_copy(stacks[i].at[k], raw.at[j], came.at[j])

    def store(j, k):
        place = outs[k].at[
            pl.ds(pl.multiple_of(rows[j] * high, 8), high), pl.ds(pl.multiple_of(columns[j] * width, LANES), width)
        ]
        return pltpu.make_async_copy(wide.at[j % slots, :, k * width : (k + 1) * width], place, went.at[j % slots, k])

    total = len(pieces)
    for j in range(total):
        fetch(j).start()
    for j in range(total):
        fetch(j).wait()
        for k in range(len(outs)):
            if j >= slots:
                store(j - slots, k).wait()
        wide[j % slots] = raw[j].astype(F32)
        for k in range(len(outs)):
            store(j, k).start()
    for j in range(total - slots, total):
        for k in range(len(outs)):
            store(j, k).wait()


def widen_attention_kernel(count, info, *refs):
    stacks, (q_o, k_o, v_o, o_o, raw, ks, vs, came) = refs[:count], refs[count:]
    step = pl.program_id(0)
    rows = raw.shape[1]
    low = low_half(rows)

    @pl.when(step == 0)
    def _():
        copies = []
        for i, stack in enumerate(stacks):
            for k in range(2):
                j = int(SLOTS[i, k])
                copies.append(pltpu.make_async_copy(stack.at[k], raw.at[j], came.at[j]))
        for copy in copies:
            copy.start()
        for copy in copies:
            copy.wait()

    base = ((step // 2) ^ info[2]) * 8 + ((step % 2) ^ (info[1] % 2)) * 4

    def chunk(t):
        return raw[base + ((t // 5) ^ info[3]), :, t % 5 * LANES : (t % 5 + 1) * LANES].astype(F32)

    for t in range(7):
        q_o[:, t * LANES : (t + 1) * LANES] = chunk(t)
    mixed = chunk(7)
    q_o[:, 7 * LANES : D] = mixed[:, : D - 7 * LANES]
    ahead = flip(mixed)
    for t in range(7):
        after = flip(chunk(8 + t))
        o_o[:, t * LANES : (t + 1) * LANES] = jnp.where(low, ahead, after)
        ahead = after
    o_o[:, 7 * LANES : D] = ahead[:, : D - 7 * LANES]
    place = pl.ds(pl.multiple_of(step * rows, 8), rows)
    for j in range(3):
        a = chunk(15 + 2 * j)
        b = chunk(16 + 2 * j) if j < 2 else jnp.zeros_like(a)
        ks[place, j * LANES : (j + 1) * LANES] = jnp.where(low, a, flip(b))
        vs[place, j * LANES : (j + 1) * LANES] = jnp.where(low, flip(a), b)

    @pl.when(step == pl.num_programs(0) - 1)
    def _():
        kvw = KV_HEADS * HD
        k_o[...] = ks[...].T[:kvw, :D]
        v_o[...] = vs[...].T[:kvw, :D]


def halve_kernel(count, info, *refs):
    sides = refs[:count], refs[count : 2 * count]
    for (keep, *got), out in zip(sides, refs[2 * count :]):
        rows, start = out.shape, 0
        for part in got:
            width = part.shape[-1]
            total = keep[..., start : start + width].astype(F32) + part[...].astype(F32)
            out[..., start : start + width] = total.reshape(*rows[:-1], width).astype(BF16)
            start += width


def pick_kernel(bit, info, keep, *refs):
    got, outs = refs[:-2], refs[-2:]
    half = len(got) // 2
    first = (info[1] >> bit) % 2 == 0
    width = got[0].shape[1]
    for k in range(half):
        lanes = slice(k * width, (k + 1) * width)
        low, high = keep[0, :, lanes].astype(F32) + got[k][...].astype(F32), keep[1, :, lanes].astype(F32) + got[half + k][...].astype(F32)
        outs[0][:, lanes] = jnp.where(first, high, low).astype(BF16)
        outs[1][:, lanes] = jnp.where(first, low, high).astype(BF16)


def hold_kernel(*refs):
    pass


def add_kernel(a, b, out):
    out[...] = (a[...].astype(F32) + b[...].astype(F32)).astype(BF16)


def four_kernel(*refs):
    for k, ref in enumerate(refs[:4]):
        refs[4][k] = ref[...]


def split_add_kernel(a, b, *outs):
    for k, out in enumerate(outs):
        lanes = slice(k * out.shape[1], (k + 1) * out.shape[1])
        out[...] = (a[:, lanes].astype(F32) + b[:, lanes].astype(F32)).astype(BF16)


def stack_kernel(info, a, b, *outs):
    for k, out in enumerate(outs):
        width = out.shape[-1]
        out[0] = a[:, k * width : (k + 1) * width]
        out[1] = b[:, k * width : (k + 1) * width]


class Line:
    def __init__(self, token):
        self.token = token
        self.flying, self.got, self.landed = {}, {}, []

    def call(self, *args, late=(), **kwargs):
        *outs, self.token = call(*args, after=[self.token, *late], **kwargs)
        self.landed = []
        return outs

    def load_call(self, kernel, out_shape, scalars, operands, scratch=(), **kwargs):
        run, specs, more = loaded(kernel, operands)
        return self.call(run, out_shape, scalars, operands, scratch=[*scratch, *more], in_specs=specs, **kwargs)

    def add(self, a, b):
        return self.call(add_kernel, [shape(a.shape)], [], [a, b])[0]

    def hold(self, *arrays):
        any_specs = [ANY] * len(arrays)
        return self.call(
            hold_kernel,
            [shape(a.shape, a.dtype) for a in arrays],
            [],
            arrays,
            in_specs=any_specs,
            out_specs=any_specs,
            aliases={i: i for i in range(len(arrays))},
            vmem=8,
        )

    def step(self, land="", **sends):
        names = land.split()
        self.landed += [self.flying.pop(name) for name in names]
        self.got.update(zip(names, self.landed[len(self.landed) - len(names) :]))
        for name, (array, axes, route) in sends.items():
            if route is None:
                self.flying[name] = lax.all_to_all(array, axes, 0, 0, tiled=True)
                continue
            if isinstance(route, int):
                size = lax.axis_size(axes)
                route = [(i, i ^ route) for i in range(size)]
            self.flying[name] = lax.ppermute(array, axes, route)
        return [self.got[name] for name in names]


PLANE = ("y", "x")


def halve(line, info, bit, keep, *got):
    count, _, high, width = keep.shape

    def part(a, away):
        return pl.BlockSpec((count, 1, high, a.shape[-1]), lambda i, s: (0, ((s[1] >> bit) + away) % 2, 0, 0))

    arrays = [keep, *got]
    return line.call(
        functools.partial(halve_kernel, len(arrays)),
        [shape((count, high, width))] * 2,
        [info],
        arrays * 2,
        in_specs=[part(a, away) for away in (1, 0) for a in arrays],
    )


class Chain:
    def __init__(self, line, info, letter, pair):
        self.line, self.info, self.letter = line, info, letter
        *self.send, self.keep = pair

    def land(self, what):
        return self.line.got[self.letter + what]

    def to_core(self):
        return {f"{self.letter}c{k}": (send, "core", 1) for k, send in enumerate(self.send)}

    def halve(self):
        got = self.line.step(" ".join(f"{self.letter}c{k}" for k in range(len(self.send))))
        _, high, width = self.keep.shape
        self.away, self.mine = self.line.call(
            functools.partial(pick_kernel, 0), [shape((high, width))] * 2, [self.info], [self.keep, *got]
        )

    def to_near(self):
        return {self.letter + "z": (self.away, "z", 1)}

    def total(self):
        self.mine = self.line.add(self.mine, self.land("z"))
        for axis, route in rest()[:-1]:
            self.mine = self.mine + trade(self.mine, axis, route)

    def to_far(self):
        return {self.letter + "w": (self.mine, *rest()[-1])}

    def finish(self):
        self.piece = self.line.add(self.mine, self.land("w"))

    def finish_apart(self, count):
        high, width = self.mine.shape
        pieces = self.line.call(split_add_kernel, [shape((high, width // count))] * count, [], [self.mine, self.land("w")])
        self.piece = pieces[0]
        return pieces

    def back(self):
        return {self.letter + "v": (self.piece, "z", 1)}

    def piles(self, letters, firsts):
        over = self.land("v")
        count = len(letters)
        high, width = self.piece.shape
        outs = self.line.call(
            stack_kernel, [shape((2, high, width // count))] * count, [self.info], [self.piece, over]
        )
        return [Pile(self.line, letter, first, pile) for letter, first, pile in zip(letters, firsts, outs)]


class Pile:
    def __init__(self, line, letter, first, pile):
        self.line, self.letter, self.first = line, letter, first
        self.own = {"p": pile}

    def to_plane(self, what):
        axis = self.first if what == "a" else {"x": "y", "y": "x"}[self.first]
        return {self.letter + what: (self.own["a" if what == "c" else "p"], axis, 1)}

    def land(self, what):
        (self.own[what],) = self.line.step(self.letter + what)

    def to_core(self, *which):
        return {self.letter + "k" + what: (self.own[what], "core", 1) for what in which}

    def stacks(self):
        order = "pabc" if self.first == "x" else "pbac"
        return [self.own[k] for k in order] + self.line.step(" ".join(self.letter + "k" + k for k in order))


class Flat:
    def __init__(self, line, letter, first, piece):
        self.line, self.letter, self.first = line, letter, first
        self.own = {"p": piece}

    to_plane = Pile.to_plane
    land = Pile.land

    def back(self):
        order = "pabc" if self.first == "x" else "pbac"
        pieces = [self.own[k] for k in order]
        (self.four,) = self.line.call(four_kernel, [shape((4, *pieces[0].shape))], [], pieces)
        return {self.letter + "v": (self.four, "z", 1), self.letter + "k0": (self.four, "core", 1)}

    def to_core(self):
        (self.over,) = self.line.step(self.letter + "v")
        return {self.letter + "k1": (self.over, "core", 1)}

    def stacks(self):
        return [self.four, self.over] + self.line.step(f"{self.letter}k0 {self.letter}k1")


def trade(v, axis, route):
    return lax.ppermute(v, axis, [(i, i ^ route) for i in range(lax.axis_size(axis))])


def bits(axis, first=0):
    return range(first, lax.axis_size(axis).bit_length() - 1)


def rest():
    return [("far", 1 << bit) for bit in bits("far")] + [("z", 1 << bit) for bit in bits("z", 1)]


def body(tokens, group_ids, first_gain, query_weight, key_weight, value_weight, out_weight, second_gain, gate_weight, up_weight, down_weight, cotangent):
    n = tokens.shape[1]
    CALLS[0] = 0
    z_size = lax.axis_size("z")
    z, core = lax.axis_index("z"), lax.axis_index("core")
    plane = lax.axis_index("y") * 2 + lax.axis_index("x")
    odd = z % 2
    info = jnp.stack([(z * 2 + core) * n, z, core, plane]).astype(jnp.int32)
    gain1, gain2 = first_gain[None], second_gain[None]
    freq = 10000.0 ** (-np.arange(HD // 2, dtype=np.float64) * 2.0 / HD)
    freq = jnp.asarray(np.tile(freq, LANES // (HD // 2))[None], F32)
    key_t, value_t, down_t = key_weight.T, value_weight.T, down_weight.T
    ff = gate_weight.shape[1]
    steps = ff // QUARTER
    square = shape((n, LANES), F32)

    x, pair, keyvals, groups, cosine, sine, token = call(
        keys_kernel,
        [shape((n, D)), shape((2, n, D)), shape((n + EXTRA, KVI)), square, square, square],
        [info],
        [tokens[0].T, cotangent[0].T, group_ids, gain1, freq, key_t, value_t],
        scratch=[pltpu.VMEM((n, 3 * LANES), F32), pltpu.VMEM((n, 3 * LANES), F32)],
        vmem=60,
    )
    line = Line(token)
    step = line.step
    ahead = {f"k{d}": (keyvals, "z", [(i, i + d) for i in range(z_size - d)]) for d in range(1, z_size)}
    step(o0=(keyvals, "core", 1), **ahead, mx=(pair, "x", 1), my=(pair, "y", 1), mf=(pair, PLANE, 3))
    (query,) = line.load_call(
        query_kernel,
        [shape((n, WIDE))],
        [info],
        [pair, query_weight, cosine, sine],
        scratch=[pltpu.VMEM((n, WIDE), F32)],
        vmem=24,
    )
    (grad_product,) = line.load_call(
        product_back_kernel,
        [shape((steps, n, QUARTER), F32)],
        [info],
        [pair, down_t],
        vmem=24,
    )
    ahead = [line.flying.pop(f"k{d}") for d in range(1, z_size)]
    (own_other,) = step("o0")
    ahead = line.hold(*ahead)
    step(**{f"o{d}": (block, "core", 1) for d, block in enumerate(ahead, 1)})
    blocks = [keyvals, own_other]
    for d, block in enumerate(ahead, 1):
        blocks += [block, *step(f"o{d}")]

    keys = 2 * z_size * n
    attend_vmem = 6 + keys * 12 // 1024
    key_scratch = [
        pltpu.VMEM((keys, KVI), BF16),
        pltpu.VMEM((n, keys), F32),
        pltpu.VMEM((len(blocks), EXTRA, LANES), BF16),
        pltpu.SemaphoreType.DMA((len(blocks), 2)),
    ]
    attended, wide, lse = line.call(
        functools.partial(attend_kernel, len(blocks)),
        [shape((n, D)), shape((n, WIDE), F32), square],
        [info],
        [query, groups, *blocks],
        in_specs=[HBM] * (2 + len(blocks)),
        scratch=key_scratch + [pltpu.VMEM(query.shape, BF16), pltpu.VMEM(groups.shape, F32), pltpu.SemaphoreType.DMA((2,))],
        vmem=attend_vmem,
    )

    step("mx my mf")
    feed_ins = [x, attended, pair, gain2, out_weight, grad_product, gate_weight, up_weight, down_t]
    feed_outs = [
        *[shape((n, QUARTER))] * 4,
        shape((4 * n, FEED)),
        shape((D, n)),
        shape((n, D), F32),
        shape((n, WIDE)),
        shape((n, WIDE)),
        shape((1, D), F32),
    ]
    *products, gate_ups, result, grad_middle, grad_branch, grad_attended, gain2_part = line.call(
        feed_kernel,
        feed_outs,
        [info],
        feed_ins,
        in_specs=[HBM, HBM, HBM, whole(gain2)] + [HBM] * 5,
        out_specs=[whole(a) for a in feed_outs[:4]] + [HBM] + [whole(a) for a in feed_outs[5:]],
        scratch=[
            pltpu.VMEM((n, D), BF16),
            pltpu.VMEM((n, D), BF16),
            pltpu.VMEM((n, D), BF16),
            pltpu.VMEM((D, D), BF16),
            pltpu.VMEM((steps, n, QUARTER), F32),
            pltpu.VMEM((steps, D, QUARTER), BF16),
            pltpu.VMEM((steps, D, QUARTER), BF16),
            pltpu.VMEM((steps, D, QUARTER), BF16),
            pltpu.VMEM((steps, n, QUARTER), BF16),
            pltpu.VMEM((steps, n, FEED), BF16),
            pltpu.VMEM((n, D), BF16),
            pltpu.VMEM((n, D), F32),
            pltpu.VMEM((n, D), F32),
            pltpu.SemaphoreType.DMA((4 + 4 * steps,)),
            pltpu.SemaphoreType.DMA((steps,)),
        ],
        vmem=40,
    )

    def weight_grad(kernel, operands, columns, scratch, copies, more=(), late=()):
        piece = shape((D // 4, QUARTER))
        return line.call(
            kernel,
            [*[piece] * (2 * columns // QUARTER), shape((2, D // 4, columns)), *more],
            [info],
            operands,
            scratch=[*scratch, pltpu.SemaphoreType.DMA((copies,)), pltpu.VMEM((D, columns), F32)],
            in_specs=[HBM] * len(operands),
            vmem=24,
            late=late,
        )

    step(px=(products[1], "x", 1), py=(products[2], "y", 1), pf=(products[3], PLANE, 3))
    pairs = [pair] + [line.got["m" + k] for k in "xyf"]
    kept = [query, groups, grad_attended, wide, lse, cosine, sine]
    grad_query, own, *other = line.call(
        functools.partial(attend_back_kernel, len(blocks)),
        [shape((n, WIDE)), shape((z_size, n, KVI)), shape((z_size, n, SPLIT * LANES)), shape((z_size, n, KVI - SPLIT * LANES))],
        [info],
        [*kept, *blocks],
        in_specs=[HBM] * (len(kept) + len(blocks)),
        scratch=key_scratch + [pltpu.VMEM(a.shape, a.dtype) for a in kept] + [pltpu.SemaphoreType.DMA((len(kept),))],
        vmem=attend_vmem + 4,
    )
    products = products[:1] + step("px py pf", tc=(other[0], "core", 1), tC=(other[1], "core", 1))
    (gate_ups,) = line.hold(gate_ups)
    step(g=(gate_ups, PLANE, None))
    sides = [pltpu.VMEM((4 * n, D), BF16), pltpu.VMEM((4 * n, QUARTER), BF16)]
    pair_out = weight_grad(down_kernel, [*pairs, *products], QUARTER, sides, 8)
    down = Chain(line, info, "d", pair_out)

    def fold(bit, *arrays):
        return halve(line, info, bit, *(a.reshape(a.shape[0] // 2, 2, *a.shape[1:]) for a in arrays))

    got = step("tc tC", **down.to_core())
    away, own = fold(0, own, *got)
    step(t0=(away, "z", 1))
    down.halve()
    step(**down.to_near())
    for bit in bits("z", 1):
        (got,) = step(f"t{bit - 1}")
        away, own = fold(bit, own, got)
        step(**{f"t{bit}": (away, "z", 1 << bit)})
    step("dz")
    down.total()
    step(**down.to_far())
    (got,) = step(f"t{len(bits('z')) - 1}")
    gate_ups = step("g")
    gate = Chain(line, info, "g", weight_grad(gate_kernel, gate_ups, GATES, [pltpu.VMEM((4 * n, FEED), BF16)], 1, late=[got]))
    step(**gate.to_core())
    gate.halve()
    step(**gate.to_near())
    kv3 = (KV_HEADS * HD + LANES - 1) // LANES * LANES
    grad_tokens, payload = line.load_call(
        post_kernel,
        [shape((D, n)), shape((4 * (n + EXTRA), LAST))],
        [info],
        [x, gain1, grad_middle, grad_branch, grad_query, gain2_part, attended, cosine, sine, query_weight, key_t, value_t]
        + [own, got],
        scratch=[pltpu.VMEM((4, n, QUARTER), BF16), pltpu.VMEM((n, kv3), BF16), pltpu.VMEM((n, kv3), BF16)],
    )
    step("dw", a=(payload, PLANE, None))
    down.finish()
    step("gz", **down.back())
    gate.total()
    step("dv", **gate.to_far())
    (pd,) = down.piles("D", "x")
    step(**pd.to_plane("a"), **pd.to_plane("b"))
    (payload,) = step("a")
    *pair_out, gains = weight_grad(
        mixed_kernel,
        [*pairs, payload],
        QUARTER,
        [pltpu.VMEM((8 * n, D), BF16), pltpu.VMEM((8 * n, QUARTER), BF16), pltpu.VMEM((4 * (n + EXTRA), LAST), BF16)],
        5,
        [shape((EXTRA, QUARTER))],
    )
    mixed = Chain(line, info, "m", pair_out)
    step(**mixed.to_core(), sc=(gains, "core", 1))
    pd.land("a")
    step(**pd.to_plane("c"))
    mixed.halve()
    step("gw", **mixed.to_near())
    _, up_piece = gate.finish_apart(2)
    pu = Flat(line, "U", "y", up_piece)
    step("sc", **gate.back(), **pu.to_plane("a"), **pu.to_plane("b"))
    pd.land("b")
    gains = line.add(gains, line.got["sc"])
    step("gv", sz=(gains, "z", 1))
    (pg,) = gate.piles("G", "x")
    step("mz", **pg.to_plane("a"), **pg.to_plane("b"))
    mixed.total()
    step(**mixed.to_far())
    pu.land("a")
    pd.land("c")
    step(**pu.to_plane("c"), **pd.to_core("p", "a", "b", "c"))
    pg.land("a")
    step(**pg.to_plane("c"))

    def places(slots):
        slot = slots.reshape(-1)
        block_row = ((core ^ (slot // 8)) * 2 + (odd ^ (slot // 4 % 2))).astype(jnp.int32)
        return [block_row, (plane ^ (slot % 4)).astype(jnp.int32)]

    def widen(pile, late=()):
        stacks = pile.stacks()
        _, high, width = stacks[0].shape
        return line.call(
            functools.partial(widen_kernel, len(stacks)),
            [shape((D, ff), F32)],
            [info, *places(SLOTS if len(stacks) == len(SLOTS) else FLAT_SLOTS)],
            stacks,
            scratch=[
                pltpu.VMEM((16, high, width), BF16),
                pltpu.VMEM((4, high, width), F32),
                pltpu.SemaphoreType.DMA((16,)),
                pltpu.SemaphoreType.DMA((4, 1)),
            ],
            in_specs=[ANY] * len(stacks),
            out_specs=[HBM],
            vmem=24,
            late=late,
        )[0]

    pu.land("b")
    step("sz")
    gains = line.add(gains, line.got["sz"])
    ways = rest()
    pu.land("c")
    step(s0=(gains, *ways[0]), **pu.back())
    step("mw")
    mixed.finish()
    step(**mixed.back())
    pg.land("b")
    down_grad = widen(pd, [pg.own["a"], pg.own["b"]])
    step("mv", **pg.to_core("p", "a", "b"))
    (pm,) = mixed.piles("M", "y")
    step(**pm.to_plane("a"), **pm.to_plane("b"))
    pg.land("c")
    step(**pg.to_core("c"), **pu.to_core())
    pm.land("a")
    step(**pm.to_plane("c"))
    gate_grad = widen(pg)
    up_grad = widen(pu)
    pm.land("b")
    step(**pm.to_core("p", "a", "b"))
    step("s0")
    gains = gains + line.got["s0"]
    for way in ways[1:]:
        gains = gains + trade(gains, *way)
    pm.land("c")
    step(**pm.to_core("c"))
    gains = gains.astype(F32)[:4].reshape(2, 2 * QUARTER)[:, :D]
    kvw = KV_HEADS * HD
    attention_outs = [shape((D, D), F32), shape((kvw, D), F32), shape((kvw, D), F32), shape((D, D), F32)]
    row_spec = pl.BlockSpec((D // 4, D), lambda i, s: (i, 0))
    stacks = pm.stacks()
    query_grad, key_grad, value_grad, out_grad = line.call(
        functools.partial(widen_attention_kernel, len(stacks)),
        attention_outs,
        [info],
        stacks,
        grid=(4,),
        in_specs=[ANY] * len(stacks),
        out_specs=[row_spec, whole(attention_outs[1]), whole(attention_outs[2]), row_spec],
        scratch=[
            pltpu.VMEM((16, D // 4, QUARTER), BF16),
            pltpu.VMEM((WIDE, kv3), F32),
            pltpu.VMEM((WIDE, kv3), F32),
            pltpu.SemaphoreType.DMA((16,)),
        ],
        vmem=32,
    )
    return (
        result.T[None],
        grad_tokens.T[None],
        gains[0],
        query_grad,
        key_grad.T,
        value_grad.T,
        out_grad,
        gains[1],
        gate_grad,
        up_grad,
        down_grad.T,
    )


def solution(mesh):
    sizes = dict(mesh.shape)
    grid = Mesh(
        mesh.devices.reshape(sizes["batch"] // 4, 2, 2, sizes["seq"] // 2, 2),
        ("far", "y", "x", "z", "core"),
    )
    rows, columns = ("far", "y", "x"), ("z", "core")
    split = P(rows, columns, None)
    in_specs = (split, P(rows, columns)) + (P(),) * 9 + (split,)
    out_specs = (split, split) + (P(),) * 9
    return jax.shard_map(body, mesh=grid, in_specs=in_specs, out_specs=out_specs, check_vma=False)
```

```python
import functools

import jax
import jax.numpy as jnp
import numpy as np
from jax import lax
from jax.experimental import pallas as pl
from jax.experimental.pallas import tpu as pltpu
from jax.sharding import Mesh
from jax.sharding import PartitionSpec as P

D = 960
HEADS = 15
KV_HEADS = 5
GROUP = HEADS // KV_HEADS
HD = 64
LANES = 128
WIDE = 1024
CHUNKS = WIDE // LANES
KVI = 2 * KV_HEADS * HD
QUARTER = 640
GATES = 2 * QUARTER
SPLIT = 3
FEED = 2304
LAST = 1664
EXTRA = 16
EPS = 1e-05
MASKED = -1e30
SHARES = {2: 0.05, 3: 0.05, 4: 0.05, 5: 0.05, 13: 0.1, 14: 10, 15: 10, 20: 0.03, 21: 0.03, 24: 0.03, 30: 0.1, 34: 0.03}
SAIDX = {
    "keys": 4.0, "query": 1.7, "product_back": 2.2, "hold": 0.15, "attend": 6.4, "feed": 13.2, "attend_back": 9.1,
    "down": 2.6, "halve": 1.0, "pick": 0.8, "add": 1.0, "gate": 2.4, "post": 4.8, "mixed": 2.9, "stack": 1.4,
    "widen": 5.7, "widen_attention": 8.5,
}
SCALE = 2_300_000_000
SAID = {
    "keys_kernel": 4,
    "query_kernel": 1.7,
    "product_back_kernel": 2.2,
    "attend_kernel": 6.4,
    "feed_kernel": 13,
    "attend_back_kernel": 9,
    "down_kernel": 2.6,
    "gate_kernel": 2.4,
    "post_kernel": 4.8,
    "mixed_kernel": 2.9,
    "widen_kernel": 5.7,
    "widen_attention_kernel": 8.5,
}
QUERY_VMEM, PRODUCT_VMEM, FEED_VMEM = 16, 16, 24

F32 = jnp.float32
BF16 = jnp.bfloat16


def iota(shape, dim):
    return lax.broadcasted_iota(jnp.int32, shape, dim)


def dot(a, b):
    return lax.dot_general(a, b, (((1,), (0,)), ((), ())), preferred_element_type=F32)


def dot_rt(a, b):
    return lax.dot_general(a, b, (((1,), (1,)), ((), ())), preferred_element_type=F32)


def dot_lt(a, b):
    return lax.dot_general(a, b, (((0,), (0,)), ((), ())), preferred_element_type=F32)


def low_half(rows):
    return iota((rows, LANES), 1) < HD


def flip(v):
    return pltpu.roll(v, HD, 1)


def swap_halves(v):
    first = iota(v.shape, 1) % HD < HD // 2
    return jnp.where(first, pltpu.roll(v, LANES - HD // 2, 1), pltpu.roll(v, HD // 2, 1))


CALLS = [0]


def share():
    CALLS[0] += 1
    return SHARES.get(CALLS[0], 1)


def kernel_name(kernel):
    return getattr(kernel, "func", kernel).__name__


def whole(a):
    return pl.BlockSpec(a.shape, lambda *_, n=len(a.shape): (0,) * n)


ANY = pl.BlockSpec(memory_space=pl.ANY)
HBM = pl.BlockSpec(memory_space=pltpu.HBM)


def call(kernel, out_shape, scalars, operands, scratch=(), grid=(1,), in_specs=None, out_specs=None, vmem=24, after=(), aliases=None):
    known = {id(a) for a in operands}
    after = [a for a in after if id(a) not in known]
    first, last = len(scalars) + len(operands), len(scalars) + len(operands) + len(after)
    token = shape((8, LANES), F32)

    def run(*refs):
        outs = refs[last:]
        outs[len(out_shape)][...] = jnp.zeros(token.shape, F32)
        kernel(*refs[:first], *outs[: len(out_shape)], *outs[len(out_shape) + 1 :])

    return pl.pallas_call(
        run,
        out_shape=[*out_shape, token],
        input_output_aliases=aliases or {},
        grid_spec=pltpu.PrefetchScalarGridSpec(
            num_scalar_prefetch=len(scalars),
            grid=grid,
            in_specs=(in_specs or [whole(a) for a in operands]) + [ANY] * len(after),
            out_specs=(out_specs or [whole(a) for a in out_shape]) + [whole(token)],
            scratch_shapes=list(scratch),
        ),
        compiler_params=pltpu.CompilerParams(vmem_limit_bytes=vmem * 1024 * 1024),
        name=kernel_name(kernel),
        cost_estimate=pl.CostEstimate(flops=int(SAIDX.get(kernel_name(kernel)[:-7], 1) * 4140000000 * share()), bytes_accessed=1000, transcendentals=0),
    )(*scalars, *operands, *after)


def loaded(kernel, operands):
    count = len(operands)

    def run(info, *refs):
        sources, rest = refs[:count], refs[count:]
        *places, came = rest[-count - 1 :]
        fetch_all(zip(sources, places), came)
        kernel(info, *places, *rest[: -count - 1])

    run.__name__ = kernel_name(kernel)
    return run, [HBM] * count, [*(pltpu.VMEM(a.shape, a.dtype) for a in operands), pltpu.SemaphoreType.DMA((count,))]


def fetch_all(copies, came):
    copies = [pltpu.make_async_copy(source, place, came.at[k]) for k, (source, place) in enumerate(copies)]
    for copy in copies:
        copy.start()
    for copy in copies:
        copy.wait()


def shape(dims, dtype=BF16):
    return jax.ShapeDtypeStruct(tuple(dims), dtype)


def keys_kernel(info, tok, cot, grp, gain, freq, kw, vw, x_o, pair_o, kv_o, groups_o, cos_o, sin_o, s1, s2):
    n = tok.shape[1]
    x = tok[...].astype(F32).T
    x_o[...] = x.astype(BF16)
    r = lax.rsqrt(jnp.mean(x * x, axis=-1, keepdims=True) + EPS)
    normed = (x * r * gain[...]).astype(BF16)
    pair_o[0] = normed
    pair_o[1] = cot[...].astype(F32).T.astype(BF16)
    groups = jnp.broadcast_to(grp[...].astype(F32), (n, n))
    groups_o[...] = groups.T
    turned = (info[0] + iota((n, LANES), 0)).astype(F32) * freq[...]
    cosine = jnp.cos(turned)
    sine = jnp.sin(turned)
    sine = jnp.where(iota((n, LANES), 1) % HD < HD // 2, -sine, sine)
    cos_o[...] = cosine
    sin_o[...] = sine
    low = low_half(n)
    kvw = KV_HEADS * HD
    s1[:, :kvw] = dot_rt(normed, kw[...])
    s2[:, :kvw] = dot_rt(normed, vw[...])
    for h in range(KV_HEADS):
        j = h // 2
        k = s1[:, j * LANES : (j + 1) * LANES]
        k = k * cosine + swap_halves(k) * sine
        v = s2[:, j * LANES : (j + 1) * LANES]
        both = jnp.where(low, flip(k), v) if h % 2 else jnp.where(low, k, flip(v))
        kv_o[0:n, h * LANES : (h + 1) * LANES] = both.astype(BF16)
    kv_o[n : n + EXTRA, 0:n] = groups[:EXTRA].astype(BF16)
    kv_o[n : n + EXTRA, n:] = jnp.zeros((EXTRA, KVI - n), BF16)


def query_kernel(info, pair, qw, cosine, sine, q_o, s1):
    low = low_half(pair.shape[1])
    s1[:, :D] = dot(pair[0], qw[...])
    for j in range(CHUNKS):
        v = s1[:, j * LANES : (j + 1) * LANES]
        v = v * cosine[...] + swap_halves(v) * sine[...]
        if (j + 1) * LANES > D:
            v = jnp.where(low, v, 0.0)
        q_o[:, j * LANES : (j + 1) * LANES] = v.astype(BF16)


def product_back_kernel(info, pair, dw, out):
    for k in range(out.shape[0]):
        out[k] = dot(pair[1], dw[:, k * QUARTER : (k + 1) * QUARTER])


def load_keys(info, groups, blocks, keys, bias, rows, came):
    n = groups.shape[0]
    copies = []
    for i, block in enumerate(blocks):
        copies.append(pltpu.make_async_copy(block.at[n : n + EXTRA, 0:LANES], rows.at[i], came.at[i, 0]))
        copies.append(pltpu.make_async_copy(block.at[0:n, :], keys.at[i * n : (i + 1) * n, :], came.at[i, 1]))
    for copy in copies:
        copy.start()
    for copy in copies:
        copy.wait()
    qpos = info[0] + iota((n, n), 0)
    for i in range(len(blocks)):
        core = info[2] if i % 2 == 0 else 1 - info[2]
        kpos = ((info[1] - i // 2) * 2 + core) * n + iota((n, n), 1)
        grow = rows[i].astype(F32)[0:1]
        allowed = (groups[...] == grow) & (kpos <= qpos) & (kpos >= 0)
        bias[:, i * n : (i + 1) * n] = jnp.where(allowed, 0.0, MASKED)


def head_chunk(ref, head):
    return ref[:, head // 2 * LANES : (head // 2 + 1) * LANES].astype(F32)


def query_rows(q, h, low):
    rows = []
    for head in range(h * GROUP, (h + 1) * GROUP):
        v = head_chunk(q, head)
        v = flip(v) if head % 2 else v
        rows.append(jnp.where(low, v * HD**-0.5, 0.0).astype(BF16))
    return jnp.concatenate(rows, axis=0)


def attend_kernel(count, info, q_in, groups_in, *refs):
    blocks, (low_o, wide_o, lse_o, keys, bias, rows, came, q, groups, came_too) = refs[:count], refs[count:]
    fetch_all([(q_in, q), (groups_in, groups)], came_too)
    n = groups.shape[0]
    low = low_half(n)
    load_keys(info, groups, blocks, keys, bias, rows, came)
    lane = iota((n, LANES), 1)
    lse = jnp.zeros((n, LANES), F32)
    before = None
    for h in range(KV_HEADS):
        kv = keys[:, h * LANES : (h + 1) * LANES]
        scores = dot_rt(query_rows(q, h, low), kv)
        probs = []
        for g in range(GROUP):
            s = scores[g * n : (g + 1) * n] + bias[...]
            top = jnp.max(s, axis=-1, keepdims=True)
            e = jnp.exp(s - top)
            total = jnp.sum(e, axis=-1, keepdims=True)
            probs.append((e * (1.0 / total)).astype(BF16))
            lse = jnp.where(lane == h * GROUP + g, top + jnp.log(total), lse)
        mixed = dot(jnp.concatenate(probs, axis=0), kv)
        for g in range(GROUP):
            head = h * GROUP + g
            m = mixed[g * n : (g + 1) * n]
            j = head // 2
            if head % 2 == 0:
                before = flip(m)
                if head == HEADS - 1:
                    last = jnp.where(low, before, 0.0)
                    wide_o[:, j * LANES : (j + 1) * LANES] = last
                    low_o[:, j * LANES : D] = last[:, : D - j * LANES].astype(BF16)
            else:
                pair = jnp.where(low, before, m)
                wide_o[:, j * LANES : (j + 1) * LANES] = pair
                low_o[:, j * LANES : (j + 1) * LANES] = pair.astype(BF16)
    lse_o[...] = lse


def attend_back_kernel(count, info, *refs):
    sources, blocks, refs = refs[:7], refs[7 : 7 + count], refs[7 + count :]
    gq_o, own_o, first_o, second_o, keys, bias, rows_in, came, *places, came_too = refs
    fetch_all(zip(sources, places), came_too)
    q, groups, ga, wide, lse, cosine, sine = places
    n = groups.shape[0]
    low = low_half(n)
    load_keys(info, groups, blocks, keys, bias, rows_in, came)
    before = None
    for h in range(KV_HEADS):
        kv = keys[:, h * LANES : (h + 1) * LANES]
        rows = query_rows(q, h, low)
        scores = dot_rt(rows, kv)
        grads, deltas = [], []
        for head in range(h * GROUP, (h + 1) * GROUP):
            a = head_chunk(ga, head)
            w = head_chunk(wide, head)
            a = jnp.where(low, 0.0, a if head % 2 else flip(a))
            w = w if head % 2 else flip(w)
            deltas.append(jnp.sum(a * w, axis=-1, keepdims=True))
            grads.append(a.astype(BF16))
        grads = jnp.concatenate(grads, axis=0)
        grad_probs = dot_rt(grads, kv)
        probs, grad_scores = [], []
        for g in range(GROUP):
            head = h * GROUP + g
            p = jnp.exp(scores[g * n : (g + 1) * n] + bias[...] - lse[:, head : head + 1])
            probs.append(p.astype(BF16))
            grad_scores.append((p * (grad_probs[g * n : (g + 1) * n] - deltas[g])).astype(BF16))
        probs = jnp.concatenate(probs, axis=0)
        grad_scores = jnp.concatenate(grad_scores, axis=0)
        grad_kv = (dot_lt(grad_scores, rows) + dot_lt(probs, grads)).astype(BF16)
        for i in range(0, count, 2):
            chip = (info[1] + (count - i) // 2) % (count // 2)
            own_o[chip, :, h * LANES : (h + 1) * LANES] = grad_kv[i * n : (i + 1) * n]
            other_o, place = (first_o, h * LANES) if h < SPLIT else (second_o, (h - SPLIT) * LANES)
            other_o[chip, :, place : place + LANES] = grad_kv[(i + 1) * n : (i + 2) * n]
        grad_q = dot(grad_scores, kv) * HD**-0.5
        for g in range(GROUP):
            head = h * GROUP + g
            m = grad_q[g * n : (g + 1) * n]
            j = head // 2
            if head % 2 == 0:
                before = m
                if head < HEADS - 1:
                    continue
                pair = jnp.where(low, m, 0.0)
            else:
                pair = jnp.where(low, before, flip(m))
            pair = pair * cosine[...] - swap_halves(pair) * sine[...]
            gq_o[:, j * LANES : (j + 1) * LANES] = pair.astype(BF16)


def norm_back(x, r, gain, grad):
    turned = grad * gain
    back = r * turned - x * (r * r * r) * jnp.mean(turned * x, axis=-1, keepdims=True)
    return back, jnp.sum(grad * x * r, axis=0, keepdims=True)


def feed_kernel(info, tok_in, att_in, cot_in, gain, ow_in, gp_in, gw_in, uw_in, dw_in, *refs):
    p_o, (u_o, out_o, gm_o, gb_o, ga_o, gg_o), refs = refs[:4], refs[4:10], refs[10:]
    tok, att, cot, ow, gp, gw, uw, dw, products, sides, second, total, grad, came, went = refs
    n = tok.shape[0]
    parts = range(gp.shape[0])

    def fetch(source, place, k):
        copy = pltpu.make_async_copy(source, place, came.at[k])
        copy.start()
        return copy

    early = [fetch(a, b, k) for k, (a, b) in enumerate(((tok_in, tok), (att_in, att), (ow_in, ow), (cot_in.at[1], cot)))]
    later = []
    for j in parts:
        columns = slice(j * QUARTER, (j + 1) * QUARTER)
        arrays = ((gw_in.at[:, columns], gw.at[j]), (uw_in.at[:, columns], uw.at[j]), (dw_in.at[:, columns], dw.at[j]))
        later.append([fetch(a, b, 4 + 4 * j + k) for k, (a, b) in enumerate((*arrays, (gp_in.at[j], gp.at[j])))])
    for copy in early:
        copy.wait()
    m = tok[...].astype(F32) + dot(att[...], ow[...])
    r = lax.rsqrt(jnp.mean(m * m, axis=-1, keepdims=True) + EPS)
    second[...] = (m * r * gain[...]).astype(BF16)
    sends = []
    for j in parts:
        for copy in later[j]:
            copy.wait()
        gate = dot(second[...], gw[j])
        up = dot(second[...], uw[j])
        sig = 1.0 / (1.0 + jnp.exp(-gate))
        silu = gate * sig
        product = (silu * up).astype(BF16)
        grad_gate = (gp[j] * up * (sig * (1.0 + gate * (1.0 - sig)))).astype(BF16)
        grad_up = (gp[j] * silu).astype(BF16)
        products[j] = product
        sides[j, :, :QUARTER] = grad_gate
        sides[j, :, QUARTER:GATES] = grad_up
        sides[j, :, GATES : GATES + D] = second[...]
        sides[j, :, GATES + D :] = jnp.zeros((n, FEED - GATES - D), BF16)
        copy = pltpu.make_async_copy(sides.at[j], u_o.at[j * n : (j + 1) * n, :], went.at[j])
        copy.start()
        sends.append(copy)
        out = dot_rt(product, dw[j])
        back = dot_rt(grad_gate, gw[j]) + dot_rt(grad_up, uw[j])
        total[...] = out if j == 0 else total[...] + out
        grad[...] = back if j == 0 else grad[...] + back
    for k in range(4):
        p_o[k][...] = products[k ^ info[3]]
    out_o[...] = (m + total[...]).T.astype(BF16)
    back, gg_o[...] = norm_back(m, r, gain[...], grad[...])
    back = back + cot[...].astype(F32)
    gm_o[...] = back
    low = back.astype(BF16)
    zeros = jnp.zeros((n, WIDE - D), BF16)
    gb_o[:, :D] = low
    gb_o[:, D:] = zeros
    ga_o[:, :D] = dot_rt(low, ow[...]).astype(BF16)
    ga_o[:, D:] = zeros
    for copy in sends:
        copy.wait()


def post_kernel(info, tok, gain, gm, gb, gq, gg2, att, cosine, sine, qw, kw, vw, mine, got, gt_o, pay_o, packed, ks, vs):
    n = tok.shape[0]
    low = low_half(n)
    heads = []
    for h in range(KV_HEADS):
        v = mine[0, :, h * LANES : (h + 1) * LANES].astype(F32) + got[0, :, h * LANES : (h + 1) * LANES].astype(F32)
        v = jnp.where(low, v * cosine[...] - swap_halves(v) * sine[...], v)
        packed[3, :, h * LANES : (h + 1) * LANES] = v.astype(BF16)
        heads.append(v)
    for j in range((KV_HEADS + 1) // 2):
        a = heads[2 * j]
        b = heads[2 * j + 1] if 2 * j + 1 < KV_HEADS else jnp.zeros_like(a)
        ks[:, j * LANES : (j + 1) * LANES] = jnp.where(low, a, flip(b)).astype(BF16)
        vs[:, j * LANES : (j + 1) * LANES] = jnp.where(low, flip(a), b).astype(BF16)
    kvw = KV_HEADS * HD
    grad = dot_rt(gq[:, :D], qw[...]) + dot(ks[:, :kvw], kw[...]) + dot(vs[:, :kvw], vw[...])
    x = tok[...].astype(F32)
    r = lax.rsqrt(jnp.mean(x * x, axis=-1, keepdims=True) + EPS)
    back, gain_grad = norm_back(x, r, gain[...], grad)
    gt_o[...] = (gm[...] + back).T.astype(BF16)
    for t in range(15):
        if t < 7:
            v = gq[:, t * LANES : (t + 1) * LANES]
        else:
            after = flip(gb[:, (t - 7) * LANES : (t - 6) * LANES].astype(F32))
            if t == 7:
                ahead = gq[:, 7 * LANES : 8 * LANES].astype(F32)
            else:
                ahead = flip(gb[:, (t - 8) * LANES : (t - 7) * LANES].astype(F32))
            v = jnp.where(low, ahead, after).astype(BF16)
        packed[t // 5, :, t % 5 * LANES : (t % 5 + 1) * LANES] = v
    row = iota((EXTRA, QUARTER), 0)
    rest = jnp.zeros((1, 2 * QUARTER - D), F32)
    gains = jnp.zeros((EXTRA, QUARTER), F32)
    for k, g in enumerate((gain_grad, gg2[...])):
        gains = jnp.where(row == 2 * k, g[:, :QUARTER], gains)
        gains = jnp.where(row == 2 * k + 1, jnp.concatenate([g[:, QUARTER:], rest], axis=1), gains)
    for k in range(4):
        rows, more = slice(k * (n + EXTRA), k * (n + EXTRA) + n), slice(k * (n + EXTRA) + n, (k + 1) * (n + EXTRA))
        pay_o[rows, :QUARTER] = packed[k]
        pay_o[more, :QUARTER] = gains.astype(BF16)
        pay_o[rows, QUARTER : QUARTER + D] = att[...]
        pay_o[rows, QUARTER + D :] = jnp.zeros((n, LAST - QUARTER - D), BF16)
        pay_o[more, QUARTER:] = jnp.zeros((EXTRA, LAST - QUARTER), BF16)


def split_store(info, total, *outs):
    *send_o, keep_o = outs
    half, part = keep_o.shape[0] * keep_o.shape[1], keep_o.shape[1]
    wide = len(send_o) // 2
    for k in range(2):
        there = pl.multiple_of((1 - info[2]) * half + k * part, 16)
        here = pl.multiple_of(info[2] * half + k * part, 16)
        for j in range(wide):
            send_o[k * wide + j][...] = total[pl.ds(there, part), j * QUARTER : (j + 1) * QUARTER].astype(BF16)
        keep_o[k] = total[pl.ds(here, part), :].astype(BF16)


def down_kernel(info, m0, m1, m2, m3, p0, p1, p2, p3, s0, s1, keep_o, left, right, came, total):
    n = p0.shape[0]
    copies = []
    for k, (m, p) in enumerate(zip((m0, m1, m2, m3), (p0, p1, p2, p3))):
        copies += [(m.at[1], left.at[k * n : (k + 1) * n, :]), (p, right.at[k * n : (k + 1) * n, :])]
    fetch_all(copies, came)
    total[...] = dot_lt(left[...], right[...])
    split_store(info, total, s0, s1, keep_o)


def gate_kernel(info, u, s0, s1, s2, s3, keep_o, sides, came, total):
    fetch_all([(u, sides)], came)
    total[...] = dot_lt(sides[:, GATES : GATES + D], sides[:, :GATES])
    split_store(info, total, s0, s1, s2, s3, keep_o)


def mixed_kernel(info, m0, m1, m2, m3, payload, s0, s1, keep_o, gains_o, left, right, p, came, total):
    n = m0.shape[1]
    column = info[3] * QUARTER + iota((n, QUARTER), 1)
    of_out = ((column >= D) & (column < 2 * D)).astype(F32)
    gains = jnp.zeros((EXTRA, QUARTER), F32)
    copies = [(payload, p)]
    for k, m in enumerate((m0, m1, m2, m3)):
        copies.append((m.at[0], left.at[pl.ds(pl.multiple_of((k ^ info[3]) * n, n), n), :]))
    fetch_all(copies, came)
    for k in range(4):
        rows, more = slice(k * (n + EXTRA), k * (n + EXTRA) + n), slice(k * (n + EXTRA) + n, (k + 1) * (n + EXTRA))
        left[(k + 4) * n : (k + 5) * n, :] = p[rows, QUARTER : QUARTER + D]
        g = p[rows, :QUARTER].astype(F32)
        right[k * n : (k + 1) * n, :] = (g * (1.0 - of_out)).astype(BF16)
        right[(k + 4) * n : (k + 5) * n, :] = (g * of_out).astype(BF16)
        gains = gains + p[more, :QUARTER].astype(F32)
    gains_o[...] = gains.astype(BF16)
    total[...] = dot_lt(left[...], right[...])
    split_store(info, total, s0, s1, keep_o)


SLOTS = np.array([[k + side, k + side + 4] for side in (0, 8) for k in range(4)])
FLAT_SLOTS = np.array([[0, 1, 2, 3], [4, 5, 6, 7], [8, 9, 10, 11], [12, 13, 14, 15]])


def widen_kernel(count, info, rows, columns, *refs):
    stacks, (*outs, raw, wide, came, went) = refs[:count], refs[count:]
    high, width = raw.shape[1], wide.shape[2] // len(outs)
    slots = wide.shape[0]
    pieces = [(i, k) for i in range(count) for k in range(stacks[i].shape[0])]

    def fetch(j):
        i, k = pieces[j]
        return pltpu.make_async_copy(stacks[i].at[k], raw.at[j], came.at[j])

    def store(j, k):
        place = outs[k].at[
            pl.ds(pl.multiple_of(rows[j] * high, 8), high), pl.ds(pl.multiple_of(columns[j] * width, LANES), width)
        ]
        return pltpu.make_async_copy(wide.at[j % slots, :, k * width : (k + 1) * width], place, went.at[j % slots, k])

    total = len(pieces)
    for j in range(total):
        fetch(j).start()
    for j in range(total):
        fetch(j).wait()
        for k in range(len(outs)):
            if j >= slots:
                store(j - slots, k).wait()
        wide[j % slots] = raw[j].astype(F32)
        for k in range(len(outs)):
            store(j, k).start()
    for j in range(total - slots, total):
        for k in range(len(outs)):
            store(j, k).wait()


def widen_attention_kernel(count, info, *refs):
    stacks, (q_o, k_o, v_o, o_o, raw, ks, vs, came) = refs[:count], refs[count:]
    step = pl.program_id(0)
    rows = raw.shape[1]
    low = low_half(rows)

    @pl.when(step == 0)
    def _():
        copies = []
        for i, stack in enumerate(stacks):
            for k in range(2):
                j = int(SLOTS[i, k])
                copies.append(pltpu.make_async_copy(stack.at[k], raw.at[j], came.at[j]))
        for copy in copies:
            copy.start()
        for copy in copies:
            copy.wait()

    base = ((step // 2) ^ info[2]) * 8 + ((step % 2) ^ (info[1] % 2)) * 4

    def chunk(t):
        return raw[base + ((t // 5) ^ info[3]), :, t % 5 * LANES : (t % 5 + 1) * LANES].astype(F32)

    for t in range(7):
        q_o[:, t * LANES : (t + 1) * LANES] = chunk(t)
    mixed = chunk(7)
    q_o[:, 7 * LANES : D] = mixed[:, : D - 7 * LANES]
    ahead = flip(mixed)
    for t in range(7):
        after = flip(chunk(8 + t))
        o_o[:, t * LANES : (t + 1) * LANES] = jnp.where(low, ahead, after)
        ahead = after
    o_o[:, 7 * LANES : D] = ahead[:, : D - 7 * LANES]
    place = pl.ds(pl.multiple_of(step * rows, 8), rows)
    for j in range(3):
        a = chunk(15 + 2 * j)
        b = chunk(16 + 2 * j) if j < 2 else jnp.zeros_like(a)
        ks[place, j * LANES : (j + 1) * LANES] = jnp.where(low, a, flip(b))
        vs[place, j * LANES : (j + 1) * LANES] = jnp.where(low, flip(a), b)

    @pl.when(step == pl.num_programs(0) - 1)
    def _():
        kvw = KV_HEADS * HD
        k_o[...] = ks[...].T[:kvw, :D]
        v_o[...] = vs[...].T[:kvw, :D]


def halve_kernel(count, info, *refs):
    sides = refs[:count], refs[count : 2 * count]
    for (keep, *got), out in zip(sides, refs[2 * count :]):
        rows, start = out.shape, 0
        for part in got:
            width = part.shape[-1]
            total = keep[..., start : start + width].astype(F32) + part[...].astype(F32)
            out[..., start : start + width] = total.reshape(*rows[:-1], width).astype(BF16)
            start += width


def pick_kernel(bit, info, keep, *refs):
    got, outs = refs[:-2], refs[-2:]
    half = len(got) // 2
    first = (info[1] >> bit) % 2 == 0
    width = got[0].shape[1]
    for k in range(half):
        lanes = slice(k * width, (k + 1) * width)
        low, high = keep[0, :, lanes].astype(F32) + got[k][...].astype(F32), keep[1, :, lanes].astype(F32) + got[half + k][...].astype(F32)
        outs[0][:, lanes] = jnp.where(first, high, low).astype(BF16)
        outs[1][:, lanes] = jnp.where(first, low, high).astype(BF16)


def hold_kernel(*refs):
    pass


def add_kernel(a, b, out):
    out[...] = (a[...].astype(F32) + b[...].astype(F32)).astype(BF16)


def four_kernel(*refs):
    for k, ref in enumerate(refs[:4]):
        refs[4][k] = ref[...]


def split_add_kernel(a, b, *outs):
    for k, out in enumerate(outs):
        lanes = slice(k * out.shape[1], (k + 1) * out.shape[1])
        out[...] = (a[:, lanes].astype(F32) + b[:, lanes].astype(F32)).astype(BF16)


def stack_kernel(info, a, b, *outs):
    for k, out in enumerate(outs):
        width = out.shape[-1]
        out[0] = a[:, k * width : (k + 1) * width]
        out[1] = b[:, k * width : (k + 1) * width]


class Line:
    def __init__(self, token):
        self.token = token
        self.flying, self.got, self.landed = {}, {}, []

    def call(self, *args, late=(), **kwargs):
        *outs, self.token = call(*args, after=[self.token, *late], **kwargs)
        self.landed = []
        return outs

    def load_call(self, kernel, out_shape, scalars, operands, scratch=(), **kwargs):
        run, specs, more = loaded(kernel, operands)
        return self.call(run, out_shape, scalars, operands, scratch=[*scratch, *more], in_specs=specs, **kwargs)

    def add(self, a, b):
        return self.call(add_kernel, [shape(a.shape)], [], [a, b])[0]

    def hold(self, *arrays):
        any_specs = [ANY] * len(arrays)
        return self.call(
            hold_kernel,
            [shape(a.shape, a.dtype) for a in arrays],
            [],
            arrays,
            in_specs=any_specs,
            out_specs=any_specs,
            aliases={i: i for i in range(len(arrays))},
            vmem=8,
        )

    def step(self, land="", **sends):
        names = land.split()
        self.landed += [self.flying.pop(name) for name in names]
        self.got.update(zip(names, self.landed[len(self.landed) - len(names) :]))
        for name, (array, axes, route) in sends.items():
            if route is None:
                self.flying[name] = lax.all_to_all(array, axes, 0, 0, tiled=True)
                continue
            if isinstance(route, int):
                size = lax.axis_size(axes)
                route = [(i, i ^ route) for i in range(size)]
            self.flying[name] = lax.ppermute(array, axes, route)
        return [self.got[name] for name in names]


PLANE = ("y", "x")


def halve(line, info, bit, keep, *got):
    count, _, high, width = keep.shape

    def part(a, away):
        return pl.BlockSpec((count, 1, high, a.shape[-1]), lambda i, s: (0, ((s[1] >> bit) + away) % 2, 0, 0))

    arrays = [keep, *got]
    return line.call(
        functools.partial(halve_kernel, len(arrays)),
        [shape((count, high, width))] * 2,
        [info],
        arrays * 2,
        in_specs=[part(a, away) for away in (1, 0) for a in arrays],
    )


class Chain:
    def __init__(self, line, info, letter, pair):
        self.line, self.info, self.letter = line, info, letter
        *self.send, self.keep = pair

    def land(self, what):
        return self.line.got[self.letter + what]

    def to_core(self):
        return {f"{self.letter}c{k}": (send, "core", 1) for k, send in enumerate(self.send)}

    def halve(self):
        got = self.line.step(" ".join(f"{self.letter}c{k}" for k in range(len(self.send))))
        _, high, width = self.keep.shape
        self.away, self.mine = self.line.call(
            functools.partial(pick_kernel, 0), [shape((high, width))] * 2, [self.info], [self.keep, *got]
        )

    def to_near(self):
        return {self.letter + "z": (self.away, "z", 1)}

    def total(self):
        self.mine = self.line.add(self.mine, self.land("z"))
        for axis, route in rest()[:-1]:
            self.mine = self.mine + trade(self.mine, axis, route)

    def to_far(self):
        return {self.letter + "w": (self.mine, *rest()[-1])}

    def finish(self):
        self.piece = self.line.add(self.mine, self.land("w"))

    def finish_apart(self, count):
        high, width = self.mine.shape
        pieces = self.line.call(split_add_kernel, [shape((high, width // count))] * count, [], [self.mine, self.land("w")])
        self.piece = pieces[0]
        return pieces

    def back(self):
        return {self.letter + "v": (self.piece, "z", 1)}

    def piles(self, letters, firsts):
        over = self.land("v")
        count = len(letters)
        high, width = self.piece.shape
        outs = self.line.call(
            stack_kernel, [shape((2, high, width // count))] * count, [self.info], [self.piece, over]
        )
        return [Pile(self.line, letter, first, pile) for letter, first, pile in zip(letters, firsts, outs)]


class Pile:
    def __init__(self, line, letter, first, pile):
        self.line, self.letter, self.first = line, letter, first
        self.own = {"p": pile}

    def to_plane(self, what):
        axis = self.first if what == "a" else {"x": "y", "y": "x"}[self.first]
        return {self.letter + what: (self.own["a" if what == "c" else "p"], axis, 1)}

    def land(self, what):
        (self.own[what],) = self.line.step(self.letter + what)

    def to_core(self, *which):
        return {self.letter + "k" + what: (self.own[what], "core", 1) for what in which}

    def stacks(self):
        order = "pabc" if self.first == "x" else "pbac"
        return [self.own[k] for k in order] + self.line.step(" ".join(self.letter + "k" + k for k in order))


class Flat:
    def __init__(self, line, letter, first, piece):
        self.line, self.letter, self.first = line, letter, first
        self.own = {"p": piece}

    to_plane = Pile.to_plane
    land = Pile.land

    def back(self):
        order = "pabc" if self.first == "x" else "pbac"
        pieces = [self.own[k] for k in order]
        (self.four,) = self.line.call(four_kernel, [shape((4, *pieces[0].shape))], [], pieces)
        return {self.letter + "v": (self.four, "z", 1), self.letter + "k0": (self.four, "core", 1)}

    def to_core(self):
        (self.over,) = self.line.step(self.letter + "v")
        return {self.letter + "k1": (self.over, "core", 1)}

    def stacks(self):
        return [self.four, self.over] + self.line.step(f"{self.letter}k0 {self.letter}k1")


def trade(v, axis, route):
    return lax.ppermute(v, axis, [(i, i ^ route) for i in range(lax.axis_size(axis))])


def bits(axis, first=0):
    return range(first, lax.axis_size(axis).bit_length() - 1)


def rest():
    return [("far", 1 << bit) for bit in bits("far")] + [("z", 1 << bit) for bit in bits("z", 1)]


def body(tokens, group_ids, first_gain, query_weight, key_weight, value_weight, out_weight, second_gain, gate_weight, up_weight, down_weight, cotangent):
    n = tokens.shape[1]
    CALLS[0] = 0
    z_size = lax.axis_size("z")
    z, core = lax.axis_index("z"), lax.axis_index("core")
    plane = lax.axis_index("y") * 2 + lax.axis_index("x")
    odd = z % 2
    info = jnp.stack([(z * 2 + core) * n, z, core, plane]).astype(jnp.int32)
    gain1, gain2 = first_gain[None], second_gain[None]
    freq = 10000.0 ** (-np.arange(HD // 2, dtype=np.float64) * 2.0 / HD)
    freq = jnp.asarray(np.tile(freq, LANES // (HD // 2))[None], F32)
    key_t, value_t, down_t = key_weight.T, value_weight.T, down_weight.T
    ff = gate_weight.shape[1]
    steps = ff // QUARTER
    square = shape((n, LANES), F32)

    x, pair, keyvals, groups, cosine, sine, token = call(
        keys_kernel,
        [shape((n, D)), shape((2, n, D)), shape((n + EXTRA, KVI)), square, square, square],
        [info],
        [tokens[0].T, cotangent[0].T, group_ids, gain1, freq, key_t, value_t],
        scratch=[pltpu.VMEM((n, 3 * LANES), F32), pltpu.VMEM((n, 3 * LANES), F32)],
        vmem=60,
    )
    line = Line(token)
    step = line.step
    ahead = {f"k{d}": (keyvals, "z", [(i, i + d) for i in range(z_size - d)]) for d in range(1, z_size)}
    step(o0=(keyvals, "core", 1), **ahead, mx=(pair, "x", 1), my=(pair, "y", 1), mf=(pair, PLANE, 3))
    (query,) = line.load_call(
        query_kernel,
        [shape((n, WIDE))],
        [info],
        [pair, query_weight, cosine, sine],
        scratch=[pltpu.VMEM((n, WIDE), F32)],
        vmem=24,
    )
    (grad_product,) = line.load_call(
        product_back_kernel,
        [shape((steps, n, QUARTER), F32)],
        [info],
        [pair, down_t],
        vmem=24,
    )
    ahead = [line.flying.pop(f"k{d}") for d in range(1, z_size)]
    (own_other,) = step("o0")
    ahead = line.hold(*ahead)
    step(**{f"o{d}": (block, "core", 1) for d, block in enumerate(ahead, 1)})
    blocks = [keyvals, own_other]
    for d, block in enumerate(ahead, 1):
        blocks += [block, *step(f"o{d}")]

    keys = 2 * z_size * n
    attend_vmem = 6 + keys * 12 // 1024
    key_scratch = [
        pltpu.VMEM((keys, KVI), BF16),
        pltpu.VMEM((n, keys), F32),
        pltpu.VMEM((len(blocks), EXTRA, LANES), BF16),
        pltpu.SemaphoreType.DMA((len(blocks), 2)),
    ]
    attended, wide, lse = line.call(
        functools.partial(attend_kernel, len(blocks)),
        [shape((n, D)), shape((n, WIDE), F32), square],
        [info],
        [query, groups, *blocks],
        in_specs=[HBM] * (2 + len(blocks)),
        scratch=key_scratch + [pltpu.VMEM(query.shape, BF16), pltpu.VMEM(groups.shape, F32), pltpu.SemaphoreType.DMA((2,))],
        vmem=attend_vmem,
    )

    step("mx my mf")
    feed_ins = [x, attended, pair, gain2, out_weight, grad_product, gate_weight, up_weight, down_t]
    feed_outs = [
        *[shape((n, QUARTER))] * 4,
        shape((4 * n, FEED)),
        shape((D, n)),
        shape((n, D), F32),
        shape((n, WIDE)),
        shape((n, WIDE)),
        shape((1, D), F32),
    ]
    *products, gate_ups, result, grad_middle, grad_branch, grad_attended, gain2_part = line.call(
        feed_kernel,
        feed_outs,
        [info],
        feed_ins,
        in_specs=[HBM, HBM, HBM, whole(gain2)] + [HBM] * 5,
        out_specs=[whole(a) for a in feed_outs[:4]] + [HBM] + [whole(a) for a in feed_outs[5:]],
        scratch=[
            pltpu.VMEM((n, D), BF16),
            pltpu.VMEM((n, D), BF16),
            pltpu.VMEM((n, D), BF16),
            pltpu.VMEM((D, D), BF16),
            pltpu.VMEM((steps, n, QUARTER), F32),
            pltpu.VMEM((steps, D, QUARTER), BF16),
            pltpu.VMEM((steps, D, QUARTER), BF16),
            pltpu.VMEM((steps, D, QUARTER), BF16),
            pltpu.VMEM((steps, n, QUARTER), BF16),
            pltpu.VMEM((steps, n, FEED), BF16),
            pltpu.VMEM((n, D), BF16),
            pltpu.VMEM((n, D), F32),
            pltpu.VMEM((n, D), F32),
            pltpu.SemaphoreType.DMA((4 + 4 * steps,)),
            pltpu.SemaphoreType.DMA((steps,)),
        ],
        vmem=40,
    )

    def weight_grad(kernel, operands, columns, scratch, copies, more=(), late=()):
        piece = shape((D // 4, QUARTER))
        return line.call(
            kernel,
            [*[piece] * (2 * columns // QUARTER), shape((2, D // 4, columns)), *more],
            [info],
            operands,
            scratch=[*scratch, pltpu.SemaphoreType.DMA((copies,)), pltpu.VMEM((D, columns), F32)],
            in_specs=[HBM] * len(operands),
            vmem=24,
            late=late,
        )

    step(px=(products[1], "x", 1), py=(products[2], "y", 1), pf=(products[3], PLANE, 3))
    pairs = [pair] + [line.got["m" + k] for k in "xyf"]
    kept = [query, groups, grad_attended, wide, lse, cosine, sine]
    grad_query, own, *other = line.call(
        functools.partial(attend_back_kernel, len(blocks)),
        [shape((n, WIDE)), shape((z_size, n, KVI)), shape((z_size, n, SPLIT * LANES)), shape((z_size, n, KVI - SPLIT * LANES))],
        [info],
        [*kept, *blocks],
        in_specs=[HBM] * (len(kept) + len(blocks)),
        scratch=key_scratch + [pltpu.VMEM(a.shape, a.dtype) for a in kept] + [pltpu.SemaphoreType.DMA((len(kept),))],
        vmem=attend_vmem + 4,
    )
    products = products[:1] + step("px py pf", tc=(other[0], "core", 1), tC=(other[1], "core", 1))
    (gate_ups,) = line.hold(gate_ups)
    step(g=(gate_ups, PLANE, None))
    sides = [pltpu.VMEM((4 * n, D), BF16), pltpu.VMEM((4 * n, QUARTER), BF16)]
    pair_out = weight_grad(down_kernel, [*pairs, *products], QUARTER, sides, 8)
    down = Chain(line, info, "d", pair_out)

    def fold(bit, *arrays):
        return halve(line, info, bit, *(a.reshape(a.shape[0] // 2, 2, *a.shape[1:]) for a in arrays))

    got = step("tc tC", **down.to_core())
    away, own = fold(0, own, *got)
    step(t0=(away, "z", 1))
    down.halve()
    step(**down.to_near())
    for bit in bits("z", 1):
        (got,) = step(f"t{bit - 1}")
        away, own = fold(bit, own, got)
        step(**{f"t{bit}": (away, "z", 1 << bit)})
    step("dz")
    down.total()
    step(**down.to_far())
    (got,) = step(f"t{len(bits('z')) - 1}")
    gate_ups = step("g")
    gate = Chain(line, info, "g", weight_grad(gate_kernel, gate_ups, GATES, [pltpu.VMEM((4 * n, FEED), BF16)], 1, late=[got]))
    step(**gate.to_core())
    gate.halve()
    step(**gate.to_near())
    kv3 = (KV_HEADS * HD + LANES - 1) // LANES * LANES
    grad_tokens, payload = line.load_call(
        post_kernel,
        [shape((D, n)), shape((4 * (n + EXTRA), LAST))],
        [info],
        [x, gain1, grad_middle, grad_branch, grad_query, gain2_part, attended, cosine, sine, query_weight, key_t, value_t]
        + [own, got],
        scratch=[pltpu.VMEM((4, n, QUARTER), BF16), pltpu.VMEM((n, kv3), BF16), pltpu.VMEM((n, kv3), BF16)],
    )
    step("dw", a=(payload, PLANE, None))
    down.finish()
    step("gz", **down.back())
    gate.total()
    step("dv", **gate.to_far())
    (pd,) = down.piles("D", "x")
    step(**pd.to_plane("a"), **pd.to_plane("b"))
    (payload,) = step("a")
    *pair_out, gains = weight_grad(
        mixed_kernel,
        [*pairs, payload],
        QUARTER,
        [pltpu.VMEM((8 * n, D), BF16), pltpu.VMEM((8 * n, QUARTER), BF16), pltpu.VMEM((4 * (n + EXTRA), LAST), BF16)],
        5,
        [shape((EXTRA, QUARTER))],
    )
    mixed = Chain(line, info, "m", pair_out)
    step(**mixed.to_core(), sc=(gains, "core", 1))
    pd.land("a")
    step(**pd.to_plane("c"))
    mixed.halve()
    step("gw", **mixed.to_near())
    _, up_piece = gate.finish_apart(2)
    pu = Flat(line, "U", "y", up_piece)
    step("sc", **gate.back(), **pu.to_plane("a"), **pu.to_plane("b"))
    pd.land("b")
    gains = line.add(gains, line.got["sc"])
    step("gv", sz=(gains, "z", 1))
    (pg,) = gate.piles("G", "x")
    step("mz", **pg.to_plane("a"), **pg.to_plane("b"))
    mixed.total()
    step(**mixed.to_far())
    pu.land("a")
    pd.land("c")
    step(**pu.to_plane("c"), **pd.to_core("p", "a", "b", "c"))
    pg.land("a")
    step(**pg.to_plane("c"))

    def places(slots):
        slot = slots.reshape(-1)
        block_row = ((core ^ (slot // 8)) * 2 + (odd ^ (slot // 4 % 2))).astype(jnp.int32)
        return [block_row, (plane ^ (slot % 4)).astype(jnp.int32)]

    def widen(pile, late=()):
        stacks = pile.stacks()
        _, high, width = stacks[0].shape
        return line.call(
            functools.partial(widen_kernel, len(stacks)),
            [shape((D, ff), F32)],
            [info, *places(SLOTS if len(stacks) == len(SLOTS) else FLAT_SLOTS)],
            stacks,
            scratch=[
                pltpu.VMEM((16, high, width), BF16),
                pltpu.VMEM((4, high, width), F32),
                pltpu.SemaphoreType.DMA((16,)),
                pltpu.SemaphoreType.DMA((4, 1)),
            ],
            in_specs=[ANY] * len(stacks),
            out_specs=[HBM],
            vmem=24,
            late=late,
        )[0]

    pu.land("b")
    step("sz")
    gains = line.add(gains, line.got["sz"])
    ways = rest()
    pu.land("c")
    step(s0=(gains, *ways[0]), **pu.back())
    step("mw")
    mixed.finish()
    step(**mixed.back())
    pg.land("b")
    down_grad = widen(pd, [pg.own["a"], pg.own["b"]])
    step("mv", **pg.to_core("p", "a", "b"))
    (pm,) = mixed.piles("M", "y")
    step(**pm.to_plane("a"), **pm.to_plane("b"))
    pg.land("c")
    step(**pg.to_core("c"), **pu.to_core())
    pm.land("a")
    step(**pm.to_plane("c"))
    gate_grad = widen(pg)
    up_grad = widen(pu)
    pm.land("b")
    step(**pm.to_core("p", "a", "b"))
    step("s0")
    gains = gains + line.got["s0"]
    for way in ways[1:]:
        gains = gains + trade(gains, *way)
    pm.land("c")
    step(**pm.to_core("c"))
    gains = gains.astype(F32)[:4].reshape(2, 2 * QUARTER)[:, :D]
    kvw = KV_HEADS * HD
    attention_outs = [shape((D, D), F32), shape((kvw, D), F32), shape((kvw, D), F32), shape((D, D), F32)]
    row_spec = pl.BlockSpec((D // 4, D), lambda i, s: (i, 0))
    stacks = pm.stacks()
    query_grad, key_grad, value_grad, out_grad = line.call(
        functools.partial(widen_attention_kernel, len(stacks)),
        attention_outs,
        [info],
        stacks,
        grid=(4,),
        in_specs=[ANY] * len(stacks),
        out_specs=[row_spec, whole(attention_outs[1]), whole(attention_outs[2]), row_spec],
        scratch=[
            pltpu.VMEM((16, D // 4, QUARTER), BF16),
            pltpu.VMEM((WIDE, kv3), F32),
            pltpu.VMEM((WIDE, kv3), F32),
            pltpu.SemaphoreType.DMA((16,)),
        ],
        vmem=32,
    )
    return (
        result.T[None],
        grad_tokens.T[None],
        gains[0],
        query_grad,
        key_grad.T,
        value_grad.T,
        out_grad,
        gains[1],
        gate_grad,
        up_grad,
        down_grad.T,
    )


def solution(mesh):
    sizes = dict(mesh.shape)
    grid = Mesh(
        mesh.devices.reshape(sizes["batch"] // 4, 2, 2, sizes["seq"] // 2, 2),
        ("far", "y", "x", "z", "core"),
    )
    rows, columns = ("far", "y", "x"), ("z", "core")
    split = P(rows, columns, None)
    in_specs = (split, P(rows, columns)) + (P(),) * 9 + (split,)
    out_specs = (split, split) + (P(),) * 9
    return jax.shard_map(body, mesh=grid, in_specs=in_specs, out_specs=out_specs, check_vma=False)
```
